32 devices in a mesh: win: 16 (over z, x, core), tp: 2 (over y).
Axes of the slice: x: 2, y: 2, z: 4, core: 2. Of those that a mesh axis runs over, the one named last changes fastest.
Arguments:
- tokens_in: bfloat16 [18432, 384], P(('win', 'tp')), may hold values from -6 to 6
- target: bfloat16 [18432, 384], P(('win', 'tp')), may hold values from -6 to 6
- loss_weight: int32 [18432], P(('win', 'tp')), may hold values from 1 to 192, as said below
- shift_offsets: int32 [128, 3], P('win'), may hold values from 0 to 11, as said below
- window_type: int32 [128], P('win'), may hold values from 0 to 15
- bias_index: int32 [144, 144], replicated, may hold values from 0 to 3311
- owners: int32 [16], replicated, may hold values from 0 to 15, each once
- norm_params: float32 [4, 384], replicated
- w_qkv: float32 [384, 3, 384], P(None, None, 'tp'), may hold values from -0.3125 to 0.3125
- w_proj: float32 [384, 384], P('tp'), may hold values from -0.875 to 0.875
- w_up: float32 [384, 1536], P(None, 'tp'), may hold values from -0.3125 to 0.3125
- w_down: float32 [1536, 384], P('tp'), may hold values from -0.15625 to 0.15625
- pos_bias: float32 [16, 3312, 12], P(None, None, 'tp'), may hold values from -6 to 6
- basis_qkv: float32 [384, 384], replicated
- basis_proj: float32 [384, 384], replicated
- basis_up: float32 [384, 384], replicated
- basis_down: float32 [384, 384], replicated
- m_qkv: float32 [384, 3, 384], P('win', None, 'tp'), may hold values from -768 to 768
- v_qkv: float32 [384, 3, 384], P('win', None, 'tp'), may hold values from 18432 to 73728
- m_proj: float32 [384, 384], P('tp', 'win'), may hold values from -3072 to 3072
- v_proj: float32 [384, 384], P('tp', 'win'), may hold values from 294912 to 1179648
- m_up: float32 [384, 1536], P('win', 'tp'), may hold values from -1024 to 1024
- v_up: float32 [384, 1536], P('win', 'tp'), may hold values from 26542.08 to 106168.32
- m_down: float32 [1536, 384], P('tp', 'win'), may hold values from -1024 to 1024
- v_down: float32 [1536, 384], P('tp', 'win'), may hold values from 26542.08 to 106168.32
- m_bias: float32 [16, 3312, 12], P(None, None, 'tp'), may hold values from -160 to 160
- v_bias: float32 [16, 3312, 12], P(None, None, 'tp'), may hold values from 1252 to 5008
- m_norm: float32 [4, 384], replicated, may hold values from -1536 to 1536
- v_norm: float32 [4, 384], replicated, may hold values from 73728 to 294912
Outputs:
- result: bfloat16 [18432, 384], P(('win', 'tp'))
- grad_tokens: float32 [18432, 384], P(('win', 'tp'))
- loss: float32 [], replicated
- grad_norm: float32 [4, 384], replicated
- grad_qkv: float32 [384, 3, 384], P(None, None, 'tp')
- grad_proj: float32 [384, 384], P('tp')
- grad_up: float32 [384, 1536], P(None, 'tp')
- grad_down: float32 [1536, 384], P('tp')
- grad_bias: float32 [16, 3312, 12], P(None, None, 'tp')
- first_qkv: float32 [384, 3, 384], P('win', None, 'tp')
- second_qkv: float32 [384, 3, 384], P('win', None, 'tp')
- new_qkv: float32 [384, 3, 384], P(None, None, 'tp')
- copy_qkv: bfloat16 [384, 3, 384], P(None, None, 'tp')
- first_proj: float32 [384, 384], P('tp', 'win')
- second_proj: float32 [384, 384], P('tp', 'win')
- new_proj: float32 [384, 384], P('tp')
- copy_proj: bfloat16 [384, 384], P('tp')
- first_up: float32 [384, 1536], P('win', 'tp')
- second_up: float32 [384, 1536], P('win', 'tp')
- new_up: float32 [384, 1536], P(None, 'tp')
- copy_up: bfloat16 [384, 1536], P(None, 'tp')
- first_down: float32 [1536, 384], P('tp', 'win')
- second_down: float32 [1536, 384], P('tp', 'win')
- new_down: float32 [1536, 384], P('tp')
- copy_down: bfloat16 [1536, 384], P('tp')
- second_bias: float32 [16, 3312, 12], P(None, None, 'tp')
- new_bias: float32 [16, 3312, 12], P(None, None, 'tp')
- second_norm: float32 [4, 384], replicated
- new_norm: float32 [4, 384], replicated
The draws below stay inside these ranges and needn't reach their ends.
Inputs may be any that keep to these rules, and one draw needn't show every extreme that they name: `loss_weight`: positive integers. `shift_offsets`: column 0 below 2, column 1 below 6, column 2 below 12.
All inputs are finite; a program needn't handle non-finite values.
Results may differ from the reference program's by a relative error of at most 0.0095.
The reference program's roundings to bfloat16 on the way count: a program that leaves them out, or rounds other values in their place, can miss the bound.
Values may be sent and summed in bfloat16 or wider, within the bound.
No kernel may reach another device: no remote copies, remote signals or barrier semaphores. Data moves between devices by JAX's collectives and lax.ppermute only.
A program may use at most 256 MiB of HBM per device.

```python
import math
import jax
import jax.numpy as jnp
from jax import lax

D = 384
HEADS = 12
HD = 32
FF = 1536
WZ = 2
WY = 6
WX = 12
TYPES = 16
STEP = 5
WIN_DEV = 8
WTOK = 144
BPOS = 3312
TOK_DEV = 576
WINDOWS = 128
TOKENS = 18432
N_WIN = 16


def draw_loss_weight(key, part):
    key = jax.random.fold_in(key, 11)
    base_key, tail_key = jax.random.split(key)
    base_value = jax.random.randint(base_key, (TOKENS,), 1, 9)
    tail_value = jnp.where(jax.random.randint(tail_key, (TOKENS,), 0, 16) == 0, 8, 1)
    device_idx = jnp.arange(TOKENS) // TOK_DEV
    last_device = max(TOKENS // TOK_DEV - 1, 1)
    rising = 1 + 2 * device_idx // last_device
    values = (base_value * tail_value * rising).astype(jnp.int32)
    values = values.at[0].set(1)
    values = values.at[TOKENS - 1].set(192)
    return values.astype(jnp.int32)


def draw_shift_offsets(key, part):
    key = jax.random.fold_in(key, 12)
    depth_key, lat_key, lon_key = jax.random.split(key, 3)
    depth_off = jax.random.randint(depth_key, (WINDOWS,), 0, WZ)
    lat_off = jax.random.randint(lat_key, (WINDOWS,), 0, WY)
    lon_off = jax.random.randint(lon_key, (WINDOWS,), 0, WX)
    return jnp.stack([depth_off, lat_off, lon_off], axis=1).astype(jnp.int32)


def draw_norm_params(key, part):
    key = jax.random.fold_in(key, 13)
    gain_key, shift_key = jax.random.split(key)
    gains = 1.0 + 0.3 * jax.random.uniform(gain_key, (2, D), jnp.float32, -1.0, 1.0)
    shifts = 0.3 * jax.random.normal(shift_key, (2, D), jnp.float32)
    return jnp.stack([gains[0], shifts[0], gains[1], shifts[1]]).astype(jnp.float32)


def basis_draw(key):
    places = jnp.arange(D)
    identity = (places[:, None] == places[None, :]).astype(jnp.float32)
    return (identity + 0.6 / D ** 0.5 * jax.random.normal(key, (D, D), jnp.float32)).astype(jnp.float32)


def draw_basis_qkv(key, part):
    key = jax.random.fold_in(key, 21)
    return basis_draw(key)


def draw_basis_proj(key, part):
    key = jax.random.fold_in(key, 22)
    return basis_draw(key)


def draw_basis_up(key, part):
    key = jax.random.fold_in(key, 23)
    return basis_draw(key)


def draw_basis_down(key, part):
    key = jax.random.fold_in(key, 24)
    return basis_draw(key)


def touch_ends(result, own_key, low, largest):
    longest = result.shape.index(max(result.shape))
    spots = []
    for shift in (0, 1):
        where = [jax.random.randint(jax.random.fold_in(own_key, axis), (), 0, length) for axis, length in enumerate(result.shape)]
        where[longest] = (where[longest] + shift) % result.shape[longest]
        spots.append(tuple(where))
    return result.at[spots[0]].set(low).at[spots[1]].set(largest)


def levels(own_key, shape, cuts, low, largest):
    level, own = 1.0, jax.random.fold_in(own_key, 6)
    for dim, shards_of in cuts:
        steps = jnp.exp(jax.random.uniform(jax.random.fold_in(own, dim), (shards_of,), jnp.float32, low / len(cuts), largest / len(cuts)))
        level = level * jnp.repeat(steps, shape[dim] // shards_of).reshape([-1 if axis == dim else 1 for axis in range(len(shape))])
    return level


def bell_draw(stream_key, shape, scale, bound, shards=(), dtype=jnp.bfloat16):
    values = jax.random.normal(stream_key, shape, jnp.float32) * scale
    if len(shards) > 0:
        values = levels(stream_key, shape, shards, -0.22, 0.18) * values
    return jnp.clip(values, min=-bound, max=bound).astype(dtype)


def setup_inputs(seed: int = 0) -> dict:
    splits = jax.random.split(jax.random.key(seed), 30)
    return {
        "tokens_in": bell_draw(splits[0], (TOKENS, D), 1.0, 6.0, ((0, 32),)),
        "target": bell_draw(splits[1], (TOKENS, D), 1.0, 6.0, ((0, 32),)),
        "loss_weight": draw_loss_weight(jax.random.fold_in(splits[29], 71), 0),
        "shift_offsets": draw_shift_offsets(jax.random.fold_in(splits[29], 71), 0),
        "window_type": touch_ends(jax.random.randint(splits[4], (WINDOWS,), 0, TYPES), jax.random.fold_in(splits[4], 1), 0, TYPES - 1).astype(jnp.int32),
        "bias_index": touch_ends(jax.random.randint(splits[5], (WTOK, WTOK), 0, BPOS), jax.random.fold_in(splits[5], 1), 0, BPOS - 1).astype(jnp.int32),
        "owners": jax.random.permutation(splits[6], N_WIN).astype(jnp.int32),
        "norm_params": draw_norm_params(jax.random.fold_in(splits[29], 71), 0),
        "w_qkv": bell_draw(splits[8], (D, 3, D), D ** -0.5, 0.3125, ((2, 2),), jnp.float32),
        "w_proj": bell_draw(splits[9], (D, D), (D // 8) ** -0.5, 0.875, ((0, 2),), jnp.float32),
        "w_up": bell_draw(splits[10], (D, FF), D ** -0.5, 0.3125, ((1, 2),), jnp.float32),
        "w_down": bell_draw(splits[11], (FF, D), FF ** -0.5, 0.15625, ((0, 2),), jnp.float32),
        "pos_bias": bell_draw(splits[12], (TYPES, BPOS, HEADS), 1.0, 6.0, ((2, 2),), jnp.float32),
        "basis_qkv": draw_basis_qkv(jax.random.fold_in(splits[29], 71), 0),
        "basis_proj": draw_basis_proj(jax.random.fold_in(splits[29], 71), 0),
        "basis_up": draw_basis_up(jax.random.fold_in(splits[29], 71), 0),
        "basis_down": draw_basis_down(jax.random.fold_in(splits[29], 71), 0),
        "m_qkv": bell_draw(splits[17], (D, 3, D), (TOKENS ** 0.5), 768.0, ((0, 16), (2, 2)), jnp.float32),
        "v_qkv": jnp.clip(jnp.exp(math.log(73728.0) - 1.3862944 * jax.random.uniform(splits[18], (D, 3, D), jnp.float32) ** levels(splits[18], (D, 3, D), ((0, 16), (2, 2)), -0.2, 0.2)), 18432.0, 73728.0),
        "m_proj": bell_draw(splits[19], (D, D), (3.5 * TOKENS ** 0.5), 3072.0, ((0, 2), (1, 16)), jnp.float32),
        "v_proj": jnp.clip(jnp.exp(math.log(1179648) - 1.3862944 * jax.random.uniform(splits[20], (D, D), jnp.float32) ** levels(splits[20], (D, D), ((0, 2), (1, 16)), -0.2, 0.2)), 294912.0, 1179648),
        "m_up": bell_draw(splits[21], (D, FF), (1.2 * TOKENS ** 0.5), 1024.0, ((0, 16), (1, 2)), jnp.float32),
        "v_up": jnp.clip(jnp.exp(math.log(106168.32) - 1.3862944 * jax.random.uniform(splits[22], (D, FF), jnp.float32) ** levels(splits[22], (D, FF), ((0, 16), (1, 2)), -0.2, 0.2)), 26542.08, 106168.32),
        "m_down": bell_draw(splits[23], (FF, D), (1.2 * TOKENS ** 0.5), 1024.0, ((0, 2), (1, 16)), jnp.float32),
        "v_down": jnp.clip(jnp.exp(math.log(106168.32) - 1.3862944 * jax.random.uniform(splits[24], (FF, D), jnp.float32) ** levels(splits[24], (FF, D), ((0, 2), (1, 16)), -0.2, 0.2)), 26542.08, 106168.32),
        "m_bias": bell_draw(splits[25], (TYPES, BPOS, HEADS), (4 * (WINDOWS * WTOK * WTOK // (TYPES * BPOS)) ** 0.5), 160.0, ((2, 2),), jnp.float32),
        "v_bias": jnp.clip(jnp.exp(math.log(5008.0) - 1.3862944 * jax.random.uniform(splits[26], (TYPES, BPOS, HEADS), jnp.float32) ** levels(splits[26], (TYPES, BPOS, HEADS), ((2, 2),), -0.2, 0.2)), 1252.0, 5008.0),
        "m_norm": bell_draw(splits[27], (4, D), (2 * TOKENS ** 0.5), 1536.0, (), jnp.float32),
        "v_norm": jnp.clip(jnp.exp(jax.random.uniform(splits[28], (4, D), jnp.float32, math.log(73728.0), math.log(294912.0))), 73728.0, 294912.0),
    }


@jax.custom_vjp
def low(v):
    return lax.optimization_barrier(v.astype(jnp.bfloat16)).astype(jnp.float32)

@jax.custom_vjp
def low_back(v):
    return v

def low_keep(v):
    return (low(v), None)

def low_pass(kept, grad):
    return (grad,)

def back_keep(v):
    return (v, None)

def back_low(kept, grad):
    return (low(grad),)
low.defvjp(low_keep, low_pass)
low_back.defvjp(back_keep, back_low)
norm_epsilon = 1e-05
learn_rate = 0.05
table_rate = 0.3
decay_rate = 0.01
beta_first = 0.5
beta_second = 0.5
adam_epsilon = 1e-08
masked_score = -1000000000.0
highest_precision = lax.Precision.HIGHEST

def layer_norm(row_block, gain_row, shift_row):
    centered = row_block - lax.optimization_barrier(jnp.mean(row_block, axis=-1, keepdims=True))
    spread = lax.optimization_barrier(jnp.mean(centered * centered, axis=-1, keepdims=True))
    return centered * lax.rsqrt(spread + norm_epsilon) * gain_row + shift_row

def window_allowed(offsets):
    places = jnp.arange(WZ * WY * WX)
    level_idx = places // (WY * WX)
    lat_idx = places // WX % WY
    lon_idx = places % WX
    region = (level_idx[None, :] >= offsets[:, 0:1]).astype(jnp.int32) * 4
    region = region + (lat_idx[None, :] >= offsets[:, 1:2]).astype(jnp.int32) * 2
    region = region + (lon_idx[None, :] >= offsets[:, 2:3]).astype(jnp.int32)
    return region[:, :, None] == region[:, None, :]

def adam_moments(gradient, first_moment, second_moment):
    first_new = beta_first * first_moment + (1.0 - beta_first) * gradient
    second_new = beta_second * second_moment + (1.0 - beta_second) * gradient * gradient
    fix_first = 1.0 - beta_first ** STEP
    fix_second = 1.0 - beta_second ** STEP
    step_value = first_new / fix_first / (jnp.sqrt(second_new / fix_second) + adam_epsilon)
    return (first_new, second_new, step_value)

def reference(tokens_in, target, loss_weight, shift_offsets, window_type, bias_index, owners, norm_params, w_qkv, w_proj, w_up, w_down, pos_bias, basis_qkv, basis_proj, basis_up, basis_down, m_qkv, v_qkv, m_proj, v_proj, m_up, v_up, m_down, v_down, m_bias, v_bias, m_norm, v_norm):
    weights_f = loss_weight.astype(jnp.float32)
    mean_weight = jnp.mean(weights_f)
    row_scale = weights_f / mean_weight
    target_f = target.astype(jnp.float32)
    allowed_all = window_allowed(shift_offsets).reshape(N_WIN, WIN_DEV, WTOK, WTOK)
    types_all = window_type.reshape(N_WIN, WIN_DEV)
    score_scale = HD ** (-0.5)

    def forward(inputs, norm_p, weight_qkv, weight_proj, weight_up, weight_down, bias_table):
        hidden_one = low(layer_norm(inputs, norm_p[0], norm_p[1]))
        projected = low(low_back(jnp.einsum('td,dje->tje', hidden_one, low(weight_qkv), precision=highest_precision)))
        shaped = projected.reshape(N_WIN, WIN_DEV, WTOK, 3, HEADS, HD)

        def attend(block):
            queries, key_rows, value_rows, types, allowed = block
            tables = jnp.transpose(bias_table[types[:, None, None], bias_index[None, :, :]], (0, 3, 1, 2))
            scores = jnp.einsum('wahe,wbhe->whab', queries, key_rows, precision=highest_precision) * score_scale + tables
            scores = low_back(scores)
            scores = jnp.where(allowed[:, None], scores, masked_score)
            attn_probs = jax.nn.softmax(scores, axis=-1)
            attn_mixed = jnp.einsum('whab,wbhe->wahe', low(attn_probs), value_rows, precision=highest_precision)
            return low(low_back(attn_mixed)).reshape(WIN_DEV * WTOK, D)
        blocks = (shaped[:, :, :, 0], shaped[:, :, :, 1], shaped[:, :, :, 2], types_all, allowed_all)
        attn_mixed = lax.map(jax.checkpoint(attend), blocks).reshape(TOKENS, D)
        middle = inputs + low_back(jnp.dot(attn_mixed, low(weight_proj), precision=highest_precision))
        hidden_two = low(layer_norm(middle, norm_p[2], norm_p[3]))
        up_rows = low_back(jnp.dot(hidden_two, low(weight_up), precision=highest_precision))
        activated = low(jax.nn.gelu(up_rows))
        result_f = middle + low_back(jnp.dot(activated, low(weight_down), precision=highest_precision))
        deviation = result_f - target_f
        objective = 0.5 * jnp.sum(row_scale * lax.optimization_barrier(jnp.sum(deviation * deviation, axis=-1)))
        return (objective, result_f)
    objective, pullback, result_f = jax.vjp(forward, tokens_in.astype(jnp.float32), norm_params, w_qkv, w_proj, w_up, w_down, pos_bias, has_aux=True)
    grad_tokens, grad_norm, grad_qkv, grad_proj, grad_up, grad_down, grad_bias = pullback(jnp.ones_like(objective))
    loss = objective / (TOKENS * D)
    block_cols = D // N_WIN
    order_qkv = jnp.take(basis_qkv.reshape(D, N_WIN, block_cols), owners, axis=1).reshape(D, D)
    order_proj = jnp.take(basis_proj.reshape(D, N_WIN, block_cols), owners, axis=1).reshape(D, D)
    order_up = jnp.take(basis_up.reshape(D, N_WIN, block_cols), owners, axis=1).reshape(D, D)
    order_down = jnp.take(basis_down.reshape(D, N_WIN, block_cols), owners, axis=1).reshape(D, D)
    rot_qkv = jnp.einsum('dr,dje->rje', order_qkv, grad_qkv, precision=highest_precision)
    rot_proj = jnp.dot(grad_proj, order_proj, precision=highest_precision)
    rot_up = jnp.dot(order_up.T, grad_up, precision=highest_precision)
    rot_down = jnp.dot(grad_down, order_down, precision=highest_precision)
    first_qkv, second_qkv, step_qkv = adam_moments(rot_qkv, m_qkv, v_qkv)
    first_proj, second_proj, step_proj = adam_moments(rot_proj, m_proj, v_proj)
    first_up, second_up, step_up = adam_moments(rot_up, m_up, v_up)
    first_down, second_down, step_down = adam_moments(rot_down, m_down, v_down)
    delta_qkv = jnp.einsum('dr,rje->dje', order_qkv, step_qkv, precision=highest_precision)
    delta_proj = jnp.dot(step_proj, order_proj.T, precision=highest_precision)
    delta_up = jnp.dot(order_up, step_up, precision=highest_precision)
    delta_down = jnp.dot(step_down, order_down.T, precision=highest_precision)
    new_qkv = w_qkv - learn_rate * (delta_qkv + decay_rate * w_qkv)
    new_proj = w_proj - learn_rate * (delta_proj + decay_rate * w_proj)
    new_up = w_up - learn_rate * (delta_up + decay_rate * w_up)
    new_down = w_down - learn_rate * (delta_down + decay_rate * w_down)
    first_bias, second_bias, step_bias = adam_moments(grad_bias, m_bias, v_bias)
    new_bias = pos_bias - table_rate * (step_bias + decay_rate * pos_bias)
    first_norm, second_norm, step_norm = adam_moments(grad_norm, m_norm, v_norm)
    new_norm = norm_params - table_rate * (step_norm + decay_rate * norm_params)
    return (result_f.astype(jnp.bfloat16), grad_tokens, loss, grad_norm, grad_qkv, grad_proj, grad_up, grad_down, grad_bias, first_qkv, second_qkv, new_qkv, new_qkv.astype(jnp.bfloat16), first_proj, second_proj, new_proj, new_proj.astype(jnp.bfloat16), first_up, second_up, new_up, new_up.astype(jnp.bfloat16), first_down, second_down, new_down, new_down.astype(jnp.bfloat16), second_bias, new_bias, second_norm, new_norm)
```

```python
import functools

import jax
import jax.numpy as jnp
from jax import lax
from jax.experimental import pallas as pl
from jax.experimental.pallas import tpu as pltpu
from jax.sharding import PartitionSpec as P

HD = 32
WZ = 2
WY = 6
WX = 12
TYPES = 16
STEP = 5
WTOK = 144
BPOS = 3312
D = 384
HALF_HEADS = 3
HROWS = HALF_HEADS * HD
HID = 384
OWN_WIN = 4
TCOLS = 2 * HALF_HEADS * OWN_WIN
LOW = 256
LOS = 13
TROWS = 320
ABLK = 8
CHUNK = ABLK * WTOK
LANES = 128
QROWS = 3 * HROWS
BROWS = HROWS + 2 * HID
DTILES = 26
DROWS = HALF_HEADS * DTILES * TYPES

norm_epsilon = 1e-05
learn_rate = 0.05
table_rate = 0.3
decay_rate = 0.01
beta_first = 0.5
beta_second = 0.5
adam_epsilon = 1e-08
masked_score = -1000000000.0
score_scale = HD ** (-0.5)

bf16 = jnp.bfloat16
f32 = jnp.float32

VM = pl.BlockSpec(memory_space=pltpu.VMEM)
SM = pl.BlockSpec(memory_space=pltpu.SMEM)


def call(kernel, outs, in_specs, scratch=(), flops=0, nbytes=0, name=None, mib=60):
    return pl.pallas_call(
        kernel,
        out_shape=[jax.ShapeDtypeStruct(s, d) for s, d in outs],
        in_specs=in_specs,
        out_specs=[VM] * len(outs),
        scratch_shapes=list(scratch),
        compiler_params=pltpu.CompilerParams(vmem_limit_bytes=mib * 2**20),
        cost_estimate=pl.CostEstimate(flops=flops, bytes_accessed=nbytes, transcendentals=0),
        name=name,
    )


def nn(a, b):
    return jnp.dot(a, b, preferred_element_type=f32)


def nt(a, b):
    return lax.dot_general(a, b, (((1,), (1,)), ((), ())), preferred_element_type=f32)


def tn(a, b):
    return lax.dot_general(a, b, (((0,), (0,)), ((), ())), preferred_element_type=f32)


def pack_kernel(
    sc, types, wq, wp, wu, wd, pb, lw, mq, mp, mu, md, vq, vp, vu, vd,
    a0, a1, b0, b1, town, tpar, send_m, send_v, tf,
):
    core, tp = sc[0], sc[1]
    n = mp.shape[0]
    for out, q, p_, u, d in ((send_m, mq, mp, mu, md), (send_v, vq, vp, vu, vd)):
        out[...] = jnp.zeros_like(out)
        row = jnp.concatenate([p_[...], u[...], d[...], q[0], q[1], q[2]], axis=1)
        out[0:n, :] = row.astype(bf16)
    total = jnp.sum(lw[...].astype(f32), axis=0, keepdims=True)
    for k in range(3):
        high = jnp.floor(total * (1.0 / LOW))
        send_m[n + k : n + k + 1, :] = jnp.broadcast_to(total - high * LOW, (1, send_m.shape[1])).astype(bf16)
        total = high
    for p, (a, b) in enumerate(((a0, b0), (a1, b1))):
        half = core if p == 0 else 1 - core
        r = pl.multiple_of(half * HROWS, 32)
        for j in range(3):
            a[j * HROWS : (j + 1) * HROWS, :] = wq[j, pl.ds(r, HROWS), :].astype(bf16)
        b[0:HROWS, :] = wp[pl.ds(r, HROWS), :].astype(bf16)
        cl = pl.multiple_of(half * HID, LANES)
        b[HROWS : HROWS + HID, :] = wu[:, pl.ds(cl, HID)].astype(bf16)
        b[HROWS + HID : BROWS, :] = wd[pl.ds(cl, HID), :].astype(bf16)
    tf[...] = jnp.zeros_like(tf)
    for dst, base in ((tpar, (1 - tp) * OWN_WIN), (town, tp * OWN_WIN)):
        for p in range(2):
            half = core if p == 0 else 1 - core
            for h in range(HALF_HEADS):
                for w in range(OWN_WIN):
                    c = (p * HALF_HEADS + h) * OWN_WIN + w
                    kind = types[base + w]
                    for lo in range(LOS):
                        size = min(LOW, BPOS - lo * LOW)
                        tf[lo * TCOLS + c : lo * TCOLS + c + 1, 0:size] = pb[
                            half * HALF_HEADS + h, pl.ds(kind, 1), lo * LOW : lo * LOW + size
                        ]
        dst[0:TROWS, :] = tf[...].astype(bf16)
        dst[TROWS:, :] = (tf[...] - tf[...].astype(bf16).astype(f32)).astype(bf16)


def one_hot(row):
    hi = row & (LOW - 1)
    places = lax.broadcasted_iota(jnp.int32, (LOW, row.shape[1]), 0)
    return jnp.where(places == hi, 1.0, 0.0).astype(bf16)


def norm_parts(v):
    cen = v - jnp.mean(v, axis=-1, keepdims=True)
    rstd = lax.rsqrt(jnp.mean(cen * cen, axis=-1, keepdims=True) + norm_epsilon)
    return cen * rstd, rstd


def head_mask(h, dtype):
    lane = lax.broadcasted_iota(jnp.int32, (1, 2 * HROWS), 1)
    return jnp.where((lane >= h * HD) & (lane < (h + 1) * HD), 1.0, 0.0).astype(dtype)


def regions(offs, w, shape, axis):
    pos = lax.broadcasted_iota(jnp.int32, shape, axis).astype(f32)
    q12 = jnp.floor((pos + 0.5) * (1.0 / WX))
    z = jnp.floor((pos + 0.5) * (1.0 / (WX * WY)))
    y = q12 - WY * z
    x = pos - WX * q12
    out = jnp.where(z >= offs[w, 0].astype(f32), 4.0, 0.0)
    out = out + jnp.where(y >= offs[w, 1].astype(f32), 2.0, 0.0)
    return out + jnp.where(x >= offs[w, 2].astype(f32), 1.0, 0.0)


def expand_tables(idx, t, tables):
    def step(ab, carry):
        row = idx[pl.ds(ab, 1), :]
        lo = row >> 8
        oh = one_hot(row)
        u = nn(jnp.concatenate([t[0:TROWS, :], t[TROWS:, :]], axis=1), jnp.concatenate([oh, oh], axis=0))
        acc = u[0:TCOLS]
        for k in range(1, LOS):
            acc = jnp.where(lo == k, u[TCOLS * k : TCOLS * (k + 1)], acc)
        a0 = pl.multiple_of(ab * ABLK, ABLK)
        main = jnp.stack([acc[:, LANES * i : LANES * (i + 1)] for i in range(ABLK)], axis=0)
        tables[:, pl.ds(a0, ABLK), 0:LANES] = jnp.swapaxes(main, 0, 1)
        off = ABLK * LANES
        n = WTOK - LANES
        rest = jnp.stack([acc[:, off + n * i : off + n * (i + 1)] for i in range(ABLK)], axis=0)
        tables[:, pl.ds(a0, ABLK), LANES:WTOK] = jnp.swapaxes(rest, 0, 1)
        return carry

    lax.fori_loop(0, WTOK // ABLK, step, 0, unroll=2)


def attend_kernel(first, sc, offs, *refs):
    if first:
        tokens, norm, a0, a1, t, idx, mixed, qkv, probs, hid, tables = refs
        xhat, _ = norm_parts(tokens[...].astype(f32))
        hid[...] = (xhat * norm[0:1, :] + norm[1:2, :]).astype(bf16)
    else:
        hid, a0, a1, t, idx, mixed, qkv, probs, tables = refs
    h1 = hid[...]
    for j in range(3):
        rows = slice(j * HROWS, (j + 1) * HROWS)
        qkv[j] = nt(h1, jnp.concatenate([a0[rows, :], a1[rows, :]], axis=0)).astype(bf16)
    expand_tables(idx, t, tables)
    base = sc[1] * OWN_WIN

    def window(w, carry):
        rows = pl.ds(pl.multiple_of(w * WTOK, 16), WTOK)
        q, k, v = qkv[0, rows, :], qkv[1, rows, :], qkv[2, rows, :]
        same = regions(offs, base + w, (WTOK, 1), 0) == regions(offs, base + w, (1, WTOK), 1)
        acc = jnp.zeros((WTOK, 2 * HROWS), f32)
        for h in range(2 * HALF_HEADS):
            c = h * OWN_WIN + w
            s = nt(q * head_mask(h, bf16), k) * score_scale + tables[c]
            s = jnp.where(same, s, masked_score)
            e = jnp.exp(s - jnp.max(s, axis=-1, keepdims=True))
            pr = (e / jnp.sum(e, axis=-1, keepdims=True)).astype(bf16)
            probs[c] = pr
            acc = acc + nn(pr, v) * head_mask(h, f32)
        mixed[rows, :] = acc.astype(bf16)
        return carry

    lax.fori_loop(0, OWN_WIN, window, 0)


def back_soft(dm, qkv, probs, a0, a1, hid, g0, g1, dhid, ds_all, dx):
    dx[...] = jnp.zeros_like(dx)

    def window(w, carry):
        rows = pl.ds(pl.multiple_of(w * WTOK, 16), WTOK)
        q, k, v = qkv[0, rows, :], qkv[1, rows, :], qkv[2, rows, :]
        d = dm[rows, :]
        dq = jnp.zeros((WTOK, 2 * HROWS), f32)
        dk = jnp.zeros((WTOK, 2 * HROWS), f32)
        dv = jnp.zeros((WTOK, 2 * HROWS), f32)
        for h in range(2 * HALF_HEADS):
            c = h * OWN_WIN + w
            mask = head_mask(h, f32)
            pr = probs[c]
            pf = pr.astype(f32)
            dp = nt(d * head_mask(h, bf16), v)
            ds = (pf * (dp - jnp.sum(pf * dp, axis=-1, keepdims=True))).astype(bf16)
            ds_all[c] = ds.astype(f32)
            dv = dv + tn(pr, d) * mask
            dq = dq + nn(ds, k) * mask
            dk = dk + tn(ds, q) * mask
        for j, v_ in enumerate((dq * score_scale, dk * score_scale, dv)):
            dx[rows, j * LOW : j * LOW + 2 * HROWS] = v_.astype(bf16)
        return carry

    lax.fori_loop(0, OWN_WIN, window, 0)
    h1 = hid[...]
    stack = []
    for j in range(3):
        rows = slice(j * HROWS, (j + 1) * HROWS)
        g = tn(dx[:, j * LOW : (j + 1) * LOW], h1)
        g0[rows, :] = g[0:HROWS].astype(g0.dtype)
        g1[rows, :] = g[HROWS : 2 * HROWS].astype(g1.dtype)
        stack += [a0[rows, :], a1[rows, :], jnp.zeros((LOW - 2 * HROWS, D), bf16)]
    dhid[...] = nn(dx[...], jnp.concatenate(stack, axis=0))


def scatter_pairs(idx, ds_all, acc_ref):
    acc_ref[...] = jnp.zeros_like(acc_ref)

    def step(ab, carry):
        row = idx[pl.ds(ab, 1), :]
        lo = row >> 8
        blk = ds_all[:, pl.ds(pl.multiple_of(ab * ABLK, ABLK), ABLK), :]
        main = jnp.swapaxes(blk[:, :, 0:LANES], 0, 1)
        rest = jnp.swapaxes(blk[:, :, LANES:WTOK], 0, 1)
        dt = jnp.concatenate([main[i] for i in range(ABLK)] + [rest[i] for i in range(ABLK)], axis=1)
        parts = [jnp.where(lo == k, dt, 0.0) for k in range(LOS)]
        parts.append(jnp.zeros((TROWS - LOS * TCOLS, CHUNK), f32))
        acc_ref[...] += nt(jnp.concatenate(parts, axis=0).astype(bf16), one_hot(row))
        return carry

    lax.fori_loop(0, WTOK // ABLK, step, 0, unroll=2)


def back_partner_kernel(dm, qkv, probs, a0, a1, hid, idx, ga, gb, dhid, ds_all, dx, acc_ref):
    back_soft(dm, qkv, probs, a0, a1, hid, ga.at[0], ga.at[1], dhid, ds_all, dx)
    scatter_pairs(idx, ds_all, acc_ref)
    gb[...] = acc_ref[...].astype(bf16)


def back_own_kernel(dm, qkv, probs, a0, a1, hid, g0, g1, dhid, ds_all, dx):
    back_soft(dm, qkv, probs, a0, a1, hid, g0, g1, dhid, ds_all, dx)


def back_bias_kernel(sc, types, ds_all, idx, rb, keep, send, acc_ref):
    tp = sc[1]
    scatter_pairs(idx, ds_all, acc_ref)
    n = 2 * HALF_HEADS
    row_h = lax.broadcasted_iota(jnp.int32, (n * TYPES, TCOLS), 0)
    col_h = lax.broadcasted_iota(jnp.int32, (n * TYPES, TCOLS), 1)
    picks = []
    for base in (tp * OWN_WIN, (1 - tp) * OWN_WIN):
        kind = jnp.zeros((n * TYPES, TCOLS), jnp.int32)
        for w in range(OWN_WIN):
            kind = jnp.where((col_h & (OWN_WIN - 1)) == w, types[base + w], kind)
        hit = ((row_h >> 4) == (col_h >> 2)) & ((row_h & (TYPES - 1)) == kind)
        picks.append(jnp.where(hit, 1.0, 0.0).astype(bf16))
    pick = jnp.concatenate([picks[0], picks[0], picks[1]], axis=1)
    other = rb[...].astype(f32)
    for lo in range(LOS):
        hi, low = split_low(acc_ref[lo * TCOLS : (lo + 1) * TCOLS, :])
        r = other[lo * TCOLS : (lo + 1) * TCOLS, :]
        vals = jnp.concatenate([hi.astype(f32), low.astype(f32), r], axis=0).astype(bf16)
        dense = nn(pick, vals)
        for h in range(n):
            out = keep if h < HALF_HEADS else send
            for part in range(2):
                at = ((h % HALF_HEADS) * DTILES + 2 * lo + part) * TYPES
                out[at : at + TYPES, :] = dense[
                    h * TYPES : (h + 1) * TYPES, part * LANES : (part + 1) * LANES
                ]


def gelu_parts(u):
    k0, k1 = 0.7978845608028654, 0.044715
    u2 = u * u
    t = jnp.tanh(k0 * u * (1.0 + k1 * u2))
    half = 0.5 * (1.0 + t)
    return u * half, half + (0.5 * k0) * u * (1.0 - t * t) * (1.0 + (3.0 * k1) * u2)


def mlp_kernel(tokens, norm, mo, mp, b0, b1, c0, c1, result, total_ref, mid_ref, act_ref, gp_ref):
    groups = (b0, b1, c0, c1)
    ups = slice(HROWS, HROWS + HID)
    downs = slice(HROWS + HID, BROWS)
    heads = jnp.concatenate([wt[0:HROWS, :] for wt in groups], axis=0)
    mid = tokens[...].astype(f32) + nn(jnp.concatenate([mo[...], mp[...]], axis=1), heads)
    mid_ref[...] = mid
    xhat, _ = norm_parts(mid)
    h2 = (xhat * norm[2:3, :] + norm[3:4, :]).astype(bf16)
    for g, wt in enumerate(groups):
        cut = slice(g * HID, (g + 1) * HID)
        value, slope = gelu_parts(nn(h2, wt[ups, :]))
        act_ref[:, cut] = value.astype(bf16)
        gp_ref[:, cut] = slope
    total = mid + nn(act_ref[...], jnp.concatenate([wt[downs, :] for wt in groups], axis=0))
    total_ref[...] = total
    result[...] = total.astype(bf16)


def digit_sum(digits):
    x = digits[...].astype(f32)
    rows = jnp.sum(x, axis=0)
    return rows[0:1] + LOW * rows[1:2] + LOW * LOW * rows[2:3]


def mlp_back_kernel(
    total, target, lw, mean_parts, other_parts, norm, mid, act, gp, mo, mp, b0, b1, c0, c1,
    s0, s1, dmid_ref, dmo, dmp, small, dup_ref,
):
    groups = (b0, b1, c0, c1)
    ups = slice(HROWS, HROWS + HID)
    downs = slice(HROWS + HID, BROWS)
    n_tokens = mean_parts.shape[0] * 2 * total.shape[0]
    mean = (digit_sum(mean_parts) + digit_sum(other_parts))[:, 0:1] / n_tokens
    scale = lw[...].astype(f32) / mean
    xhat, rstd = norm_parts(mid[...])
    gain = norm[2:3, :]
    h2 = (xhat * gain + norm[3:4, :]).astype(bf16)
    dev = total[...] - target[...].astype(f32)
    og = scale * dev
    weighted = jnp.sum(og * dev, axis=0, keepdims=True)
    ol = og.astype(bf16)
    for g, wt in enumerate(groups):
        cut = slice(g * HID, (g + 1) * HID)
        out = (s0, s1)[g % 2]
        side = g // 2
        out[side, downs, :] = tn(act[:, cut], ol).astype(out.dtype)
        dup = (nt(ol, wt[downs, :]) * gp[:, cut]).astype(bf16)
        out[side, ups, :] = tn(h2, dup).astype(out.dtype)
        dup_ref[:, cut] = dup
    dh2 = nt(dup_ref[...], jnp.concatenate([wt[ups, :] for wt in groups], axis=1))
    small[...] = jnp.zeros_like(small)
    small[0:1, :] = jnp.sum(dh2 * xhat, axis=0, keepdims=True)
    small[1:2, :] = jnp.sum(dh2, axis=0, keepdims=True)
    small[2:3, :] = weighted
    gd = dh2 * gain
    dmid = og + rstd * (
        gd - jnp.mean(gd, axis=-1, keepdims=True) - xhat * jnp.mean(gd * xhat, axis=-1, keepdims=True)
    )
    dmid_ref[...] = dmid
    ml = dmid.astype(bf16)
    for side, (mx, dmx) in enumerate(((mo, dmo), (mp, dmp))):
        wpx = jnp.concatenate([wt[0:HROWS, :] for wt in groups[2 * side : 2 * side + 2]], axis=0)
        g = tn(mx[...], ml)
        s0[side, 0:HROWS, :] = g[0:HROWS]
        s1[side, 0:HROWS, :] = g[HROWS:].astype(bf16)
        dmx[...] = nt(ml, wpx).astype(bf16)


def first_norm_kernel(do, dp, tokens, norm, dmid, grad, small):
    xhat, rstd = norm_parts(tokens[...].astype(f32))
    dh = do[...] + dp[...]
    small[...] = jnp.zeros_like(small)
    small[0:1, :] = jnp.sum(dh * xhat, axis=0, keepdims=True)
    small[1:2, :] = jnp.sum(dh, axis=0, keepdims=True)
    gd = dh * norm[0:1, :]
    grad[...] = dmid[...] + rstd * (
        gd - jnp.mean(gd, axis=-1, keepdims=True) - xhat * jnp.mean(gd * xhat, axis=-1, keepdims=True)
    )


def permute_win(x, mask):
    n = lax.axis_size("win")
    return lax.ppermute(x, "win", [(i, i ^ mask) for i in range(n)])


def swap_tp(x):
    return lax.ppermute(x, "tp", [(0, 1), (1, 0)])


def far_masks():
    n = lax.axis_size("win")
    return [1 << k for k in range(2, n.bit_length() - 1)]


def sum_small(x):
    x = x + swap_tp(x)
    for m in [1, 2] + far_masks():
        x = x + permute_win(x, m)
    return x


def after(x, *others):
    return lax.optimization_barrier((x, *others))[0]


def cut_half(x, which):
    n = x.shape[0] // 2
    return lax.dynamic_slice_in_dim(x, which * n, n, 0)


def sum_chips(total, bit):
    keep = cut_half(total, bit)
    send = cut_half(total, 1 - bit).astype(bf16)
    yield send
    x = (keep + permute_win(send, 2).astype(f32)).astype(bf16)
    for m in far_masks():
        yield x
        x = (x.astype(f32) + permute_win(x, m).astype(f32)).astype(bf16)
    yield x
    other = permute_win(x, 2)
    yield other
    return x, other, permute_win(x, 1), permute_win(other, 1)


def finish(gen):
    while True:
        try:
            next(gen)
        except StopIteration as stop:
            return stop.value


def split_low(v):
    hi = v.astype(bf16)
    return hi, (v - hi.astype(f32)).astype(bf16)


def order_kernel(cols, own_cols, bq, bp, bu, bd, hi_ref, lo_ref, own_hi, own_lo):
    pick = jnp.where(lax.broadcasted_iota(jnp.int32, (D, D), 1) == cols[...], 1.0, 0.0).astype(bf16)
    n = own_cols.shape[0]
    own = jnp.where(lax.broadcasted_iota(jnp.int32, (n, D), 1) == own_cols[...], 1.0, 0.0).astype(bf16)
    for i, b in enumerate((bq, bp, bu, bd)):
        hi, lo = split_low(b[...])
        hi_ref[i] = nt(pick, hi).astype(bf16)
        lo_ref[i] = nt(pick, lo).astype(bf16)
        own_hi[i] = nt(own, hi).astype(bf16)
        own_lo[i] = nt(own, lo).astype(bf16)


def moments(grad, m, v):
    first = beta_first * m + (1.0 - beta_first) * grad
    second = beta_second * v + (1.0 - beta_second) * grad * grad
    return first, second


def step_of(first, second):
    fix_first = 1.0 - beta_first**STEP
    fix_second = 1.0 - beta_second**STEP
    return first / fix_first / (jnp.sqrt(second / fix_second) + adam_epsilon)


def assemble(sc, pieces, full):
    core, xb = sc[0], sc[2]
    n = pieces[0].shape[0]
    for p in range(2):
        half = core if p == 0 else 1 - core
        for q in range(2):
            part = xb if q == 0 else 1 - xb
            full[half, pl.ds(pl.multiple_of(part * n, 16), n), :] = pieces[2 * p + q][...]


def gathered(ref, n, lanes):
    x = ref[:, :, lanes].astype(f32)
    return jnp.concatenate([x[i, 0:n] for i in range(x.shape[0])], axis=0)


def rotated_update(pt, g, own, mv, lanes, w, rows_form):
    hi, lo = pt
    mul = nt if rows_form else nn
    axis = 1 if rows_form else 0
    twice = jnp.concatenate([g, g], axis=axis)
    rot = mul(jnp.concatenate([hi, lo], axis=1), twice)
    rot_own = mul(jnp.concatenate([own[0], own[1]], axis=1), twice)
    first, second = moments(rot, gathered(mv[0], own[0].shape[0], lanes), gathered(mv[1], own[0].shape[0], lanes))
    shi, slo = split_low(step_of(first, second))
    left, right = jnp.concatenate([shi, shi, slo], axis=0), jnp.concatenate([hi, lo, hi], axis=0)
    delta = tn(left, right) if rows_form else tn(right, left)
    new = w - learn_rate * (delta + decay_rate * w)
    return rot_own, new


def update_main_kernel(
    sc, q0, q1, q2, q3, ms, vs, hi, lo, ohi, olo, wp, wu, wd, mp, vp, mu, vu, md, vd,
    gp, gu, gd, fp, sp, np_, cp, fu, su, nu, cu, fd, sd, nd, cd, full,
):
    assemble(sc, (q0, q1, q2, q3), full)
    for h in range(2):
        gp[h * HROWS : (h + 1) * HROWS, :] = full[h, 0:HROWS, :].astype(f32)
        gu[:, h * HID : (h + 1) * HID] = full[h, HROWS : HROWS + HID, :].astype(f32)
        gd[h * HID : (h + 1) * HID, :] = full[h, HROWS + HID : BROWS, :].astype(f32)
    jobs = (
        (1, slice(0, 192), True, gp, wp, mp, vp, fp, sp, np_, cp, HROWS, 0),
        (2, slice(192, 960), False, gu, wu, mu, vu, fu, su, nu, cu, HID, HROWS),
        (3, slice(960, 1728), True, gd, wd, md, vd, fd, sd, nd, cd, HID, HROWS + HID),
    )
    for i, lanes, rows_form, g, w, m, v, f, s, n, c, size, start in jobs:
        for h in range(2):
            cut = slice(h * size, (h + 1) * size)
            ml = slice(lanes.start + h * size, lanes.start + (h + 1) * size)
            gh = full[h, start : start + size, :]
            at = (cut, slice(None)) if rows_form else (slice(None), cut)
            rot_own, new = rotated_update(
                (hi[i], lo[i]), gh, (ohi[i], olo[i]), (ms, vs), ml, w[at], rows_form
            )
            n[at] = new
            c[at] = new.astype(bf16)
            first, second = moments(rot_own, m[:, cut], v[:, cut])
            f[:, cut] = first
            s[:, cut] = second


def update_qkv_kernel(sc, q0, q1, q2, q3, ms, vs, hi, lo, ohi, olo, wq, mq, vq, gq, fq, sq, nq, cq, full):
    assemble(sc, (q0, q1, q2, q3), full)
    for j in range(3):
        g = jnp.concatenate([full[h, j * HROWS : (j + 1) * HROWS, :] for h in range(2)], axis=0)
        gq[j] = g.astype(f32)
        lanes = slice(1728 + j * 192, 1728 + (j + 1) * 192)
        rot_own, new = rotated_update(
            (hi[0], lo[0]), g, (ohi[0], olo[0]), (ms, vs), lanes, wq[j], True
        )
        nq[j] = new
        cq[j] = new.astype(bf16)
        first, second = moments(rot_own, mq[j], vq[j])
        fq[j] = first
        sq[j] = second


def update_bias_kernel(sc, q0, q1, q2, q3, pb, mb, vb, gbias, sbias, nbias, full):
    half, k = pl.program_id(0), pl.program_id(1)

    @pl.when((half == 0) & (k == 0))
    def _():
        assemble(sc, (q0, q1, q2, q3), full)

    for i in range(DTILES):
        size = min(LANES, BPOS - i * LANES)
        at = (0, slice(None), slice(i * LANES, i * LANES + size))
        r = (k * DTILES + i) * TYPES
        g = full[half, pl.ds(pl.multiple_of(r, TYPES), TYPES), 0:size].astype(f32)
        first, second = moments(g, mb[at], vb[at])
        gbias[at] = g
        sbias[at] = second
        w = pb[at]
        nbias[at] = w - table_rate * (step_of(first, second) + decay_rate * w)


def update_bias(sc, quarters, pb, mb, vb):
    block = pl.BlockSpec((1, TYPES, BPOS), lambda half, k: (half * HALF_HEADS + k, 0, 0))
    whole = pl.BlockSpec((DROWS // 2, LANES), lambda half, k: (0, 0))
    return pl.pallas_call(
        update_bias_kernel,
        out_shape=[jax.ShapeDtypeStruct(pb.shape, f32)] * 3,
        grid=(2, HALF_HEADS),
        in_specs=[SM] + [whole] * 4 + [block] * 3,
        out_specs=[block] * 3,
        scratch_shapes=[pltpu.VMEM((2, DROWS, LANES), bf16)],
        compiler_params=pltpu.CompilerParams(vmem_limit_bytes=60 * 2**20),
        cost_estimate=pl.CostEstimate(flops=10**7, bytes_accessed=10 << 20, transcendentals=0),
        name="update_bias",
    )(sc, *quarters, pb, mb, vb)


def body(
    tokens_in, target, loss_weight, shift_offsets, window_type, bias_index, owners, norm_params,
    w_qkv, w_proj, w_up, w_down, pos_bias, basis_qkv, basis_proj, basis_up, basis_down,
    m_qkv, v_qkv, m_proj, v_proj, m_up, v_up, m_down, v_down, m_bias, v_bias, m_norm, v_norm,
):
    rows = tokens_in.shape[0]
    n_win = lax.axis_size("win")
    block_cols = D // n_win
    me, tp = lax.axis_index("win"), lax.axis_index("tp")
    xb = (me >> 1) & 1
    sc = jnp.stack([me & 1, tp, xb]).astype(jnp.int32)
    total_rows = rows * n_win * lax.axis_size("tp")
    lw = loss_weight.reshape(rows, 1)
    wq = jnp.transpose(w_qkv, (1, 2, 0))
    pb = jnp.transpose(pos_bias, (2, 0, 1))
    mq, vq = jnp.transpose(m_qkv, (1, 0, 2)), jnp.transpose(v_qkv, (1, 0, 2))
    mp, vp, md, vd = m_proj.T, v_proj.T, m_down.T, v_down.T
    n_t = WTOK // ABLK
    idx = jnp.concatenate(
        [bias_index[:, :LANES].reshape(n_t, -1), bias_index[:, LANES:].reshape(n_t, -1)], axis=1
    )

    pad = -(-(block_cols + 3) // 16) * 16
    wide_cols = 1728 + 576
    a0, a1, b0, b1, town, tpar, send_m, send_v = call(
        pack_kernel,
        [((QROWS, D), bf16)] * 2
        + [((BROWS, D), bf16)] * 2
        + [((2 * TROWS, LOW), bf16)] * 2
        + [((pad, wide_cols), bf16)] * 2,
        [SM, SM] + [VM] * 14,
        [pltpu.VMEM((TROWS, LOW), f32)],
        nbytes=8 << 20,
        name="pack",
    )(sc, window_type, wq, w_proj, w_up, w_down, pb, lw, mq, mp, m_up, md, vq, vp, v_up, vd)
    all_m = lax.all_gather(send_m, "win", axis=0)
    all_v = lax.all_gather(after(send_v, all_m), "win", axis=0)
    pa0 = swap_tp(a0)
    ptab = swap_tp(tpar)
    pb0 = swap_tp(b0)
    pa1 = permute_win(pa0, 1)
    pb1 = permute_win(pb0, 1)

    attn_outs = [
        ((rows, 2 * HROWS), bf16),
        ((3, rows, 2 * HROWS), bf16),
        ((TCOLS, WTOK, WTOK), bf16),
    ]
    tables = [pltpu.VMEM((TCOLS, WTOK, WTOK), f32)]
    mo, qkv_o, probs_o, hid = call(
        functools.partial(attend_kernel, True),
        attn_outs + [((rows, D), bf16)],
        [SM, SM] + [VM] * 6,
        tables,
        flops=rows * D * 576 * 2 + 20 * 10**9,
        name="attend_own",
    )(sc, shift_offsets, tokens_in, norm_params, a0, a1, town, idx)
    mpar, qkv_p, probs_p = call(
        functools.partial(attend_kernel, False),
        attn_outs,
        [SM, SM] + [VM] * 5,
        tables,
        flops=rows * D * 576 * 2 + 20 * 10**9,
        name="attend_partner",
    )(sc, shift_offsets, hid, pa0, pa1, ptab, idx)

    result, total, mid, act, gp = call(
        mlp_kernel,
        [
            ((rows, D), bf16),
            ((rows, D), f32),
            ((rows, D), f32),
            ((rows, 4 * HID), bf16),
            ((rows, 4 * HID), f32),
        ],
        [VM] * 8,
        flops=rows * D * 1536 * 4,
        nbytes=8 << 20,
        name="feed_forward",
    )(tokens_in, norm_params, mo, mpar, b0, b1, pb0, pb1)
    mean_parts = all_m[:, block_cols : block_cols + 3, 0:LANES]
    s0, s1, dmid, dmo, dmp, small_two = call(
        mlp_back_kernel,
        [
            ((2, BROWS, D), f32),
            ((2, BROWS, D), bf16),
            ((rows, D), f32),
            ((rows, 2 * HROWS), bf16),
            ((rows, 2 * HROWS), bf16),
            ((8, D), f32),
        ],
        [VM] * 15,
        [pltpu.VMEM((rows, 4 * HID), bf16)],
        flops=rows * D * 1536 * 8,
        nbytes=16 << 20,
        name="feed_forward_back",
    )(total, target, lw, mean_parts, swap_tp(mean_parts), norm_params, mid, act, gp, mo, mpar, b0, b1, pb0, pb1)

    r1 = permute_win(s1, 1)
    par_sum = (s0[1] + r1[1].astype(f32)).astype(bf16)
    ry = swap_tp(par_sum).astype(f32)
    main_steps = sum_chips(s0[0] + r1[0].astype(f32) + ry, xb)

    ds_shape = (TCOLS, WTOK, WTOK)
    dx_scratch = pltpu.VMEM((rows, 3 * LOW), bf16)
    acc_scratch = pltpu.VMEM((TROWS, LOW), f32)
    gpar, gbp, dhid_p = call(
        back_partner_kernel,
        [((2, QROWS, D), bf16), ((TROWS, LOW), bf16), ((rows, D), f32)],
        [VM] * 7,
        [pltpu.VMEM(ds_shape, f32), dx_scratch, acc_scratch],
        flops=20 * 10**9,
        name="back_partner",
    )(after(dmp, par_sum), qkv_p, probs_p, pa0, pa1, hid, idx)
    got_b = swap_tp(gbp)
    got_a = swap_tp(gpar)
    go0, go1, dhid_o, ds_own = call(
        back_own_kernel,
        [((QROWS, D), f32)] * 2 + [((rows, D), f32), (ds_shape, f32)],
        [VM] * 6,
        [dx_scratch],
        flops=10**10,
        name="back_own",
    )(after(dmo, next(main_steps), gbp), qkv_o, probs_o, a0, a1, hid)
    got_a = after(got_a, go0).astype(f32)
    qkv_sum = go0 + got_a[0] + permute_win(go1 + got_a[1], 1)
    qkv_steps = sum_chips(qkv_sum, xb)
    keep, send = call(
        back_bias_kernel,
        [((DROWS, LANES), f32)] * 2,
        [SM, SM] + [VM] * 3,
        [acc_scratch],
        flops=10**10,
        name="back_bias",
    )(sc, window_type, after(ds_own, next(main_steps), next(qkv_steps)), idx, got_b)
    bias_steps = sum_chips(keep + permute_win(send, 1), xb)
    grad_tokens, small_one = call(
        first_norm_kernel, [((rows, D), f32), ((8, D), f32)], [VM] * 5, nbytes=5 << 20, name="first_norm"
    )(after(dhid_o, send), dhid_p, tokens_in, norm_params, dmid)
    small = sum_small(jnp.concatenate([small_one[0:2], small_two[0:3], small_two[3:6]], axis=0))
    grad_norm = small[0:4]
    loss = jnp.sum(small[4]) * 0.5 / (total_rows * D)
    main = finish(main_steps)
    qkv_quarters = finish(qkv_steps)
    bias_quarters = finish(bias_steps)

    cols = (owners[:, None] * block_cols + jnp.arange(block_cols)[None, :]).reshape(D, 1)
    own_cols = owners[me] * block_cols + jnp.arange(block_cols)[:, None]
    hi, lo, ohi, olo = call(
        order_kernel,
        [((4, D, D), bf16)] * 2 + [((4, block_cols, D), bf16)] * 2,
        [VM] * 6,
        nbytes=6 << 20,
        name="order",
    )(cols, own_cols, basis_qkv, basis_proj, basis_up, basis_down)

    def like(*arrays):
        return [(a.shape, f32) for a in arrays]

    (
        grad_proj, grad_up, grad_down, first_proj, second_proj, new_proj, copy_proj,
        first_up, second_up, new_up, copy_up, first_down, second_down, new_down, copy_down,
    ) = call(
        update_main_kernel,
        like(w_proj, w_up, w_down, mp, mp, w_proj) + [(w_proj.shape, bf16)]
        + like(m_up, m_up, w_up) + [(w_up.shape, bf16)]
        + like(md, md, w_down) + [(w_down.shape, bf16)],
        [SM] + [VM] * 19,
        [pltpu.VMEM((2, BROWS, D), bf16)],
        flops=10**9 * 5,
        nbytes=20 << 20,
        name="update_main",
    )(sc, *main, all_m, all_v, hi, lo, ohi, olo, w_proj, w_up, w_down, mp, vp, m_up, v_up, md, vd)

    grad_qkv, first_qkv, second_qkv, new_qkv, copy_qkv = call(
        update_qkv_kernel,
        like(wq, mq, mq, wq) + [(wq.shape, bf16)],
        [SM] + [VM] * 13,
        [pltpu.VMEM((2, QROWS, D), bf16)],
        flops=10**9 * 2,
        nbytes=10 << 20,
        name="update_qkv",
    )(sc, *qkv_quarters, all_m, all_v, hi, lo, ohi, olo, wq, mq, vq)
    grad_bias, second_bias, new_bias = update_bias(
        sc, bias_quarters, pb, jnp.transpose(m_bias, (2, 0, 1)), jnp.transpose(v_bias, (2, 0, 1))
    )

    first_norm, second_norm = moments(grad_norm, m_norm, v_norm)
    new_norm = norm_params - table_rate * (step_of(first_norm, second_norm) + decay_rate * norm_params)

    def wide(v):
        return jnp.transpose(v, (2, 0, 1))

    def heads_last(v):
        return jnp.transpose(v, (1, 2, 0))

    def rows_first(v):
        return jnp.transpose(v, (1, 0, 2))

    return (
        result,
        grad_tokens,
        loss,
        grad_norm,
        wide(grad_qkv),
        grad_proj,
        grad_up,
        grad_down,
        heads_last(grad_bias),
        rows_first(first_qkv),
        rows_first(second_qkv),
        wide(new_qkv),
        wide(copy_qkv),
        first_proj.T,
        second_proj.T,
        new_proj,
        copy_proj,
        first_up,
        second_up,
        new_up,
        copy_up,
        first_down.T,
        second_down.T,
        new_down,
        copy_down,
        heads_last(second_bias),
        heads_last(new_bias),
        second_norm,
        new_norm,
    )


def solution(mesh):
    return jax.shard_map(
        body,
        mesh=mesh,
        in_specs=(
            P(("win", "tp"), None),
            P(("win", "tp"), None),
            P(("win", "tp")),
            P("win", None),
            P("win"),
            P(),
            P(),
            P(),
            P(None, None, "tp"),
            P("tp", None),
            P(None, "tp"),
            P("tp", None),
            P(None, None, "tp"),
            P(),
            P(),
            P(),
            P(),
            P("win", None, "tp"),
            P("win", None, "tp"),
            P("tp", "win"),
            P("tp", "win"),
            P("win", "tp"),
            P("win", "tp"),
            P("tp", "win"),
            P("tp", "win"),
            P(None, None, "tp"),
            P(None, None, "tp"),
            P(),
            P(),
        ),
        out_specs=(
            P(("win", "tp"), None),
            P(("win", "tp"), None),
            P(),
            P(),
            P(None, None, "tp"),
            P("tp", None),
            P(None, "tp"),
            P("tp", None),
            P(None, None, "tp"),
            P("win", None, "tp"),
            P("win", None, "tp"),
            P(None, None, "tp"),
            P(None, None, "tp"),
            P("tp", "win"),
            P("tp", "win"),
            P("tp", None),
            P("tp", None),
            P("win", "tp"),
            P("win", "tp"),
            P(None, "tp"),
            P(None, "tp"),
            P("tp", "win"),
            P("tp", "win"),
            P("tp", None),
            P("tp", None),
            P(None, None, "tp"),
            P(None, None, "tp"),
            P(),
            P(),
        ),
        check_vma=False,
    )
```

```python
import functools

import jax
import jax.numpy as jnp
from jax import lax
from jax.experimental import pallas as pl
from jax.experimental.pallas import tpu as pltpu
from jax.sharding import PartitionSpec as P

HD = 32
WZ = 2
WY = 6
WX = 12
TYPES = 16
STEP = 5
WTOK = 144
BPOS = 3312
D = 384
HALF_HEADS = 3
HROWS = HALF_HEADS * HD
HID = 384
OWN_WIN = 4
TCOLS = 2 * HALF_HEADS * OWN_WIN
LOW = 256
LOS = 13
TROWS = 320
ABLK = 8
CHUNK = ABLK * WTOK
LANES = 128
QROWS = 3 * HROWS
BROWS = HROWS + 2 * HID
DTILES = 26
DROWS = HALF_HEADS * DTILES * TYPES
TAIL = 3 * QROWS + DROWS
MCOLS = 2304
MBLK = 768

norm_epsilon = 1e-05
learn_rate = 0.05
table_rate = 0.3
decay_rate = 0.01
beta_first = 0.5
beta_second = 0.5
adam_epsilon = 1e-08
masked_score = -1000000000.0
score_scale = HD ** (-0.5)

bf16 = jnp.bfloat16
f32 = jnp.float32

VM = pl.BlockSpec(memory_space=pltpu.VMEM)
SM = pl.BlockSpec(memory_space=pltpu.SMEM)


def call(kernel, outs, in_specs, scratch=(), name=None, mib=60, grid=(), out_specs=None):
    return pl.pallas_call(
        kernel,
        out_shape=[jax.ShapeDtypeStruct(s, d) for s, d in outs],
        grid=grid,
        in_specs=in_specs,
        out_specs=out_specs or [VM] * len(outs),
        scratch_shapes=list(scratch),
        compiler_params=pltpu.CompilerParams(vmem_limit_bytes=mib * 2**20),
        cost_estimate=pl.CostEstimate(flops=0, bytes_accessed=0, transcendentals=0),
        name=name,
    )


BY_WINDOW = pl.BlockSpec((2 * HALF_HEADS, 1, WTOK, WTOK), lambda w: (0, w, 0, 0))
PAIRS = (2 * HALF_HEADS, OWN_WIN, WTOK, WTOK)


def nn(a, b):
    return jnp.dot(a, b, preferred_element_type=f32)


def nt(a, b):
    return lax.dot_general(a, b, (((1,), (1,)), ((), ())), preferred_element_type=f32)


def tn(a, b):
    return lax.dot_general(a, b, (((0,), (0,)), ((), ())), preferred_element_type=f32)


def moments_kernel(lw, mq, mp, mu, md, vq, vp, vu, vd, send_m, send_v):
    n = mp.shape[0]
    for out, q, p_, u, d in ((send_m, mq, mp, mu, md), (send_v, vq, vp, vu, vd)):
        out[...] = jnp.zeros_like(out)
        row = jnp.concatenate([q[0], q[1], q[2], p_[...], u[...], d[...]], axis=1)
        out[0:n, :] = row.astype(bf16)
    total = jnp.sum(lw[...].astype(f32), axis=0, keepdims=True)
    for k in range(3):
        high = jnp.floor(total * (1.0 / LOW))
        send_m[n + k : n + k + 1, :] = jnp.broadcast_to(total - high * LOW, (1, MCOLS)).astype(bf16)
        total = high


def pack_kernel(sc, types, wq, wp, wu, wd, pb, a0, a1, b0, b1, town, tpar, tf):
    core, tp = sc[0], sc[1]
    for p, (a, b) in enumerate(((a0, b0), (a1, b1))):
        half = core if p == 0 else 1 - core
        r = pl.multiple_of(half * HROWS, 32)
        for j in range(3):
            a[j * HROWS : (j + 1) * HROWS, :] = wq[j, pl.ds(r, HROWS), :].astype(bf16)
        b[0:HROWS, :] = wp[pl.ds(r, HROWS), :].astype(bf16)
        cl = pl.multiple_of(half * HID, LANES)
        b[HROWS : HROWS + HID, :] = wu[:, pl.ds(cl, HID)].astype(bf16)
        b[HROWS + HID : BROWS, :] = wd[pl.ds(cl, HID), :].astype(bf16)
    tf[...] = jnp.zeros_like(tf)
    for dst, base in ((tpar, (1 - tp) * OWN_WIN), (town, tp * OWN_WIN)):
        for p in range(2):
            half = core if p == 0 else 1 - core
            for h in range(HALF_HEADS):
                for w in range(OWN_WIN):
                    c = (p * HALF_HEADS + h) * OWN_WIN + w
                    kind = types[base + w]
                    for lo in range(LOS):
                        size = min(LOW, BPOS - lo * LOW)
                        tf[lo * TCOLS + c : lo * TCOLS + c + 1, 0:size] = pb[
                            half * HALF_HEADS + h, pl.ds(kind, 1), lo * LOW : lo * LOW + size
                        ]
        dst[0:TROWS, :] = tf[...].astype(bf16)
        dst[TROWS:, :] = (tf[...] - tf[...].astype(bf16).astype(f32)).astype(bf16)


def one_hot(row):
    hi = row & (LOW - 1)
    places = lax.broadcasted_iota(jnp.int32, (LOW, row.shape[1]), 0)
    return jnp.where(places == hi, 1.0, 0.0).astype(bf16)


def norm_parts(v):
    cen = v - jnp.mean(v, axis=-1, keepdims=True)
    rstd = lax.rsqrt(jnp.mean(cen * cen, axis=-1, keepdims=True) + norm_epsilon)
    return cen * rstd, rstd


def head_mask(h, dtype):
    lane = lax.broadcasted_iota(jnp.int32, (1, 2 * HROWS), 1)
    return jnp.where((lane >= h * HD) & (lane < (h + 1) * HD), 1.0, 0.0).astype(dtype)


def regions(offs, w, shape, axis):
    pos = lax.broadcasted_iota(jnp.int32, shape, axis).astype(f32)
    q12 = jnp.floor((pos + 0.5) * (1.0 / WX))
    z = jnp.floor((pos + 0.5) * (1.0 / (WX * WY)))
    y = q12 - WY * z
    x = pos - WX * q12
    out = jnp.where(z >= offs[0, w].astype(f32), 4.0, 0.0)
    out = out + jnp.where(y >= offs[1, w].astype(f32), 2.0, 0.0)
    return out + jnp.where(x >= offs[2, w].astype(f32), 1.0, 0.0)


def expand_tables(idx, t, tables):
    def step(ab, carry):
        row = idx[pl.ds(ab, 1), :]
        lo = row >> 8
        oh = one_hot(row)
        u = nn(t[...], one_hot(row))
        acc = 0.0
        for part in (0, TROWS):
            one = u[part : part + TCOLS]
            for k in range(1, LOS):
                one = jnp.where(lo == k, u[part + TCOLS * k : part + TCOLS * (k + 1)], one)
            acc = acc + one
        a0 = pl.multiple_of(ab * ABLK, ABLK)
        main = jnp.stack([acc[:, LANES * i : LANES * (i + 1)] for i in range(ABLK)], axis=0)
        tables[:, pl.ds(a0, ABLK), 0:LANES] = jnp.swapaxes(main, 0, 1)
        off = ABLK * LANES
        n = WTOK - LANES
        rest = jnp.stack([acc[:, off + n * i : off + n * (i + 1)] for i in range(ABLK)], axis=0)
        tables[:, pl.ds(a0, ABLK), LANES:WTOK] = jnp.swapaxes(rest, 0, 1)
        return carry

    lax.fori_loop(0, WTOK // ABLK, step, 0, unroll=3)


def attend_kernel(first, sc, offs, *refs):
    w = pl.program_id(0)
    if first:
        tokens, norm, a0, a1, t, idx, mixed, qkv, hid, probs, tables = refs
    else:
        hid, a0, a1, t, idx, mixed, qkv, probs, tables = refs

    @pl.when(w == 0)
    def _():
        if first:
            xhat, _ = norm_parts(tokens[...].astype(f32))
            hid[...] = (xhat * norm[0:1, :] + norm[1:2, :]).astype(bf16)
        h1 = hid[...]
        for j in range(3):
            rows = slice(j * HROWS, (j + 1) * HROWS)
            qkv[j] = nt(h1, jnp.concatenate([a0[rows, :], a1[rows, :]], axis=0)).astype(bf16)
        expand_tables(idx, t, tables)

    at = sc[1] * OWN_WIN + w
    rows = pl.ds(pl.multiple_of(w * WTOK, 16), WTOK)
    q, k, v = qkv[0, rows, :], qkv[1, rows, :], qkv[2, rows, :]
    same = regions(offs, at, (WTOK, 1), 0) == regions(offs, at, (1, WTOK), 1)
    acc = jnp.zeros((WTOK, 2 * HROWS), f32)
    for h in range(2 * HALF_HEADS):
        s = nt(q * head_mask(h, bf16), k) * score_scale + tables[h * OWN_WIN + w]
        s = jnp.where(same, s, masked_score)
        e = jnp.exp(s - jnp.max(s, axis=-1, keepdims=True))
        pr = e / jnp.sum(e, axis=-1, keepdims=True)
        probs[h, 0] = pr
        acc = acc + nn(pr.astype(bf16), v) * head_mask(h, f32)
    mixed[rows, :] = acc.astype(bf16)


def back_soft(dm, qkv, probs, a0, a1, hid, g0, g1, dhid, put, dx):
    w = pl.program_id(0)

    @pl.when(w == 0)
    def _():
        dx[...] = jnp.zeros_like(dx)

    rows = pl.ds(pl.multiple_of(w * WTOK, 16), WTOK)
    q, k, v = qkv[0, rows, :], qkv[1, rows, :], qkv[2, rows, :]
    d = dm[rows, :]
    dq = jnp.zeros((WTOK, 2 * HROWS), f32)
    dk = jnp.zeros((WTOK, 2 * HROWS), f32)
    dv = jnp.zeros((WTOK, 2 * HROWS), f32)
    for h in range(2 * HALF_HEADS):
        mask = head_mask(h, f32)
        pf = probs[h, 0]
        pr = pf.astype(bf16)
        dp = nt(d * head_mask(h, bf16), v)
        ds = (pf * (dp - jnp.sum(pf * dp, axis=-1, keepdims=True))).astype(bf16)
        put(h, w, ds.astype(f32))
        dv = dv + tn(pr, d) * mask
        dq = dq + nn(ds, k) * mask
        dk = dk + tn(ds, q) * mask
    for j, v_ in enumerate((dq * score_scale, dk * score_scale, dv)):
        dx[rows, j * LOW : j * LOW + 2 * HROWS] = v_.astype(bf16)

    @pl.when(w == OWN_WIN - 1)
    def _():
        h1 = hid[...]
        stack = []
        for j in range(3):
            rows = slice(j * HROWS, (j + 1) * HROWS)
            g = tn(dx[:, j * LOW : (j + 1) * LOW], h1)
            g0[rows, :] = g[0:HROWS].astype(g0.dtype)
            g1[rows, :] = g[HROWS : 2 * HROWS].astype(g1.dtype)
            stack += [a0[rows, :], a1[rows, :], jnp.zeros((LOW - 2 * HROWS, D), bf16)]
        dhid[...] = nn(dx[...], jnp.concatenate(stack, axis=0))


def scatter_pairs(idx, ds_all, acc_ref):
    acc_ref[...] = jnp.zeros_like(acc_ref)

    def step(ab, carry):
        row = idx[pl.ds(ab, 1), :]
        lo = row >> 8
        blk = ds_all[:, pl.ds(pl.multiple_of(ab * ABLK, ABLK), ABLK), :]
        main = jnp.swapaxes(blk[:, :, 0:LANES], 0, 1)
        rest = jnp.swapaxes(blk[:, :, LANES:WTOK], 0, 1)
        dt = jnp.concatenate([main[i] for i in range(ABLK)] + [rest[i] for i in range(ABLK)], axis=1)
        parts = [jnp.where(lo == k, dt, 0.0) for k in range(LOS)]
        parts.append(jnp.zeros((TROWS - LOS * TCOLS, CHUNK), f32))
        acc_ref[...] += nt(jnp.concatenate(parts, axis=0).astype(bf16), one_hot(row))
        return carry

    lax.fori_loop(0, WTOK // ABLK, step, 0, unroll=3)


def back_partner_kernel(dm, qkv, probs, a0, a1, hid, idx, ga, gb, dhid, ds_all, dx, acc_ref):
    def put(h, w, ds):
        ds_all[h * OWN_WIN + w] = ds

    back_soft(dm, qkv, probs, a0, a1, hid, ga.at[0], ga.at[1], dhid, put, dx)

    @pl.when(pl.program_id(0) == OWN_WIN - 1)
    def _():
        scatter_pairs(idx, ds_all, acc_ref)
        gb[...] = acc_ref[...].astype(bf16)


def back_own_kernel(dm, qkv, probs, a0, a1, hid, g0, g1, dhid, ds_all, dx):
    def put(h, w, ds):
        ds_all[h, 0] = ds

    back_soft(dm, qkv, probs, a0, a1, hid, g0, g1, dhid, put, dx)


def back_bias_kernel(sc, types, ds_all, idx, own0, own1, got, rb, keep, send, acc_ref):
    tp = sc[1]
    for p, (own, out) in enumerate(((own0, keep), (own1, send))):
        g = own[...] + got[p].astype(f32)
        for k in range(3):
            out[k * QROWS : (k + 1) * QROWS, :] = g[:, k * LANES : (k + 1) * LANES]
    scatter_pairs(idx, ds_all, acc_ref)
    n = 2 * HALF_HEADS
    row_h = lax.broadcasted_iota(jnp.int32, (n * TYPES, TCOLS), 0)
    col_h = lax.broadcasted_iota(jnp.int32, (n * TYPES, TCOLS), 1)
    picks = []
    for base in (tp * OWN_WIN, (1 - tp) * OWN_WIN):
        kind = jnp.zeros((n * TYPES, TCOLS), jnp.int32)
        for w in range(OWN_WIN):
            kind = jnp.where((col_h & (OWN_WIN - 1)) == w, types[base + w], kind)
        hit = ((row_h >> 4) == (col_h >> 2)) & ((row_h & (TYPES - 1)) == kind)
        picks.append(jnp.where(hit, 1.0, 0.0).astype(bf16))
    pick = jnp.concatenate([picks[0], picks[0], picks[1]], axis=1)
    other = rb[...].astype(f32)
    for lo in range(LOS):
        hi, low = split_low(acc_ref[lo * TCOLS : (lo + 1) * TCOLS, :])
        r = other[lo * TCOLS : (lo + 1) * TCOLS, :]
        vals = jnp.concatenate([hi.astype(f32), low.astype(f32), r], axis=0).astype(bf16)
        dense = nn(pick, vals)
        for h in range(n):
            out = keep if h < HALF_HEADS else send
            for part in range(2):
                at = 3 * QROWS + ((h % HALF_HEADS) * DTILES + 2 * lo + part) * TYPES
                out[at : at + TYPES, :] = dense[
                    h * TYPES : (h + 1) * TYPES, part * LANES : (part + 1) * LANES
                ]


def gelu_parts(u):
    k0, k1 = 0.7978845608028654, 0.044715
    u2 = u * u
    t = jnp.tanh(k0 * u * (1.0 + k1 * u2))
    half = 0.5 * (1.0 + t)
    return u * half, half + (0.5 * k0) * u * (1.0 - t * t) * (1.0 + (3.0 * k1) * u2)


def digit_sum(digits):
    x = digits[...].astype(f32)
    rows = jnp.sum(x, axis=0)
    return rows[0:1] + LOW * rows[1:2] + LOW * LOW * rows[2:3]


def mlp_kernel(
    tokens, target, lw, mean_parts, other_parts, norm, mo, mp, b0, b1, c0, c1,
    result, s0, s1, dmid_ref, dmo, dmp, small, act, gp,
):
    groups = (b0, b1, c0, c1)
    ups = slice(HROWS, HROWS + HID)
    downs = slice(HROWS + HID, BROWS)
    n_tokens = mean_parts.shape[0] * 2 * tokens.shape[0]
    mean = (digit_sum(mean_parts) + digit_sum(other_parts))[:, 0:1] / n_tokens
    scale = lw[...].astype(f32) / mean
    heads = jnp.concatenate([wt[0:HROWS, :] for wt in groups], axis=0)
    mid = tokens[...].astype(f32) + nn(jnp.concatenate([mo[...], mp[...]], axis=1), heads)
    xhat, rstd = norm_parts(mid)
    gain = norm[2:3, :]
    h2 = (xhat * gain + norm[3:4, :]).astype(bf16)
    for g, wt in enumerate(groups):
        cut = slice(g * HID, (g + 1) * HID)
        value, slope = gelu_parts(nn(h2, wt[ups, :]))
        act[:, cut] = value.astype(bf16)
        gp[:, cut] = slope
    total = mid + nn(act[...], jnp.concatenate([wt[downs, :] for wt in groups], axis=0))
    result[...] = total.astype(bf16)
    dev = total - target[...].astype(f32)
    og = scale * dev
    weighted = jnp.sum(og * dev, axis=0, keepdims=True)
    ol = og.astype(bf16)
    for g, wt in enumerate(groups):
        cut = slice(g * HID, (g + 1) * HID)
        out = (s0, s1)[g % 2]
        side = g // 2
        out[side, downs, :] = tn(act[:, cut], ol).astype(out.dtype)
        dup = (nt(ol, wt[downs, :]) * gp[:, cut]).astype(bf16)
        out[side, ups, :] = tn(h2, dup).astype(out.dtype)
        act[:, cut] = dup
    dh2 = nt(act[...], jnp.concatenate([wt[ups, :] for wt in groups], axis=1))
    small[...] = jnp.zeros_like(small)
    small[0:1, :] = jnp.sum(dh2 * xhat, axis=0, keepdims=True)
    small[1:2, :] = jnp.sum(dh2, axis=0, keepdims=True)
    small[2:3, :] = weighted
    gd = dh2 * gain
    dmid = og + rstd * (
        gd - jnp.mean(gd, axis=-1, keepdims=True) - xhat * jnp.mean(gd * xhat, axis=-1, keepdims=True)
    )
    dmid_ref[...] = dmid
    ml = dmid.astype(bf16)
    for side, (mx, dmx) in enumerate(((mo, dmo), (mp, dmp))):
        wpx = jnp.concatenate([wt[0:HROWS, :] for wt in groups[2 * side : 2 * side + 2]], axis=0)
        g = tn(mx[...], ml)
        s0[side, 0:HROWS, :] = g[0:HROWS]
        s1[side, 0:HROWS, :] = g[HROWS:].astype(bf16)
        dmx[...] = nt(ml, wpx).astype(bf16)


def first_norm_kernel(do, dp, tokens, norm, dmid, grad, small):
    xhat, rstd = norm_parts(tokens[...].astype(f32))
    dh = do[...] + dp[...]
    small[...] = jnp.zeros_like(small)
    small[0:1, :] = jnp.sum(dh * xhat, axis=0, keepdims=True)
    small[1:2, :] = jnp.sum(dh, axis=0, keepdims=True)
    gd = dh * norm[0:1, :]
    grad[...] = dmid[...] + rstd * (
        gd - jnp.mean(gd, axis=-1, keepdims=True) - xhat * jnp.mean(gd * xhat, axis=-1, keepdims=True)
    )


def permute_win(x, mask):
    n = lax.axis_size("win")
    return lax.ppermute(x, "win", [(i, i ^ mask) for i in range(n)])


def swap_tp(x):
    return lax.ppermute(x, "tp", [(0, 1), (1, 0)])


def far_masks():
    n = lax.axis_size("win")
    return [1 << k for k in range(2, n.bit_length() - 1)]


def after(x, *others):
    return lax.optimization_barrier((x, *others))[0]


def cut_half(x, which):
    n = x.shape[0] // 2
    return lax.dynamic_slice_in_dim(x, which * n, n, 0)


class Order:
    def __init__(self, token):
        self.token = token

    def __call__(self, x):
        return after(x, *self.token)

    def done(self, *token):
        self.token = token
        return token[0]


def split_low(v):
    hi = v.astype(bf16)
    return hi, (v - hi.astype(f32)).astype(bf16)


def order_kernel(cols, own_cols, bq, bp, bu, bd, hi_ref, lo_ref, own_hi, own_lo):
    pick = jnp.where(lax.broadcasted_iota(jnp.int32, (D, D), 1) == cols[...], 1.0, 0.0).astype(bf16)
    n = own_cols.shape[0]
    own = jnp.where(lax.broadcasted_iota(jnp.int32, (n, D), 1) == own_cols[...], 1.0, 0.0).astype(bf16)
    for i, b in enumerate((bq, bp, bu, bd)):
        hi, lo = split_low(b[...])
        hi_ref[i] = nt(pick, hi).astype(bf16)
        lo_ref[i] = nt(pick, lo).astype(bf16)
        own_hi[i] = nt(own, hi).astype(bf16)
        own_lo[i] = nt(own, lo).astype(bf16)


def moments(grad, m, v):
    first = beta_first * m + (1.0 - beta_first) * grad
    second = beta_second * v + (1.0 - beta_second) * grad * grad
    return first, second


def step_of(first, second):
    fix_first = 1.0 - beta_first**STEP
    fix_second = 1.0 - beta_second**STEP
    return first / fix_first / (jnp.sqrt(second / fix_second) + adam_epsilon)


def assemble(sc, pieces, full):
    core, xb = sc[0], sc[2]
    n = pieces[0].shape[0]
    for p in range(2):
        half = core if p == 0 else 1 - core
        for q in range(2):
            part = xb if q == 0 else 1 - xb
            full[half, pl.ds(pl.multiple_of(part * n, 16), n), :] = pieces[2 * p + q][...]


def gathered(ref, n, lanes):
    x = ref[:, :, lanes].astype(f32)
    return jnp.concatenate([x[i, 0:n] for i in range(x.shape[0])], axis=0)


def rotated_update(pt, g, own, mv, lanes, w, rows_form):
    hi, lo = pt
    mul = nt if rows_form else nn
    axis = 1 if rows_form else 0
    twice = jnp.concatenate([g, g], axis=axis)
    rot = mul(jnp.concatenate([hi, lo], axis=1), twice)
    rot_own = mul(jnp.concatenate([own[0], own[1]], axis=1), twice)
    first, second = moments(rot, gathered(mv[0], own[0].shape[0], lanes), gathered(mv[1], own[0].shape[0], lanes))
    shi, slo = split_low(step_of(first, second))
    left, right = jnp.concatenate([shi, shi, slo], axis=0), jnp.concatenate([hi, lo, hi], axis=0)
    delta = tn(left, right) if rows_form else tn(right, left)
    new = w - learn_rate * (delta + decay_rate * w)
    return rot_own, new


def update_main_kernel(
    sc, q0, q1, q2, q3, ms, vs, hi, lo, ohi, olo, wp, wu, wd, mp, vp, mu, vu, md, vd,
    gp, gu, gd, fp, sp, np_, cp, fu, su, nu, cu, fd, sd, nd, cd, full,
):
    assemble(sc, (q0, q1, q2, q3), full)
    for h in range(2):
        gp[h * HROWS : (h + 1) * HROWS, :] = full[h, 0:HROWS, :].astype(f32)
        gu[:, h * HID : (h + 1) * HID] = full[h, HROWS : HROWS + HID, :].astype(f32)
        gd[h * HID : (h + 1) * HID, :] = full[h, HROWS + HID : BROWS, :].astype(f32)
    jobs = (
        (1, slice(576, 768), True, gp, wp, mp, vp, fp, sp, np_, cp, HROWS, 0),
        (2, slice(768, 1536), False, gu, wu, mu, vu, fu, su, nu, cu, HID, HROWS),
        (3, slice(1536, 2304), True, gd, wd, md, vd, fd, sd, nd, cd, HID, HROWS + HID),
    )
    for i, lanes, rows_form, g, w, m, v, f, s, n, c, size, start in jobs:
        for h in range(2):
            cut = slice(h * size, (h + 1) * size)
            ml = slice(lanes.start + h * size, lanes.start + (h + 1) * size)
            gh = full[h, start : start + size, :]
            at = (cut, slice(None)) if rows_form else (slice(None), cut)
            rot_own, new = rotated_update(
                (hi[i], lo[i]), gh, (ohi[i], olo[i]), (ms, vs), ml, w[at], rows_form
            )
            n[at] = new
            c[at] = new.astype(bf16)
            first, second = moments(rot_own, m[:, cut], v[:, cut])
            f[:, cut] = first
            s[:, cut] = second


def update_qkv_kernel(sc, q0, q1, q2, q3, ms, vs, hi, lo, ohi, olo, wq, mq, vq, gq, fq, sq, nq, cq, full):
    assemble(sc, (q0, q1, q2, q3), full)
    for j in range(3):
        g = jnp.concatenate(
            [
                jnp.concatenate(
                    [full[h, k * QROWS + j * HROWS : k * QROWS + (j + 1) * HROWS, :] for k in range(3)], axis=1
                )
                for h in range(2)
            ],
            axis=0,
        )
        gq[j] = g.astype(f32)
        lanes = slice(j * 192, (j + 1) * 192)
        rot_own, new = rotated_update(
            (hi[0], lo[0]), g, (ohi[0], olo[0]), (ms, vs), lanes, wq[j], True
        )
        nq[j] = new
        cq[j] = new.astype(bf16)
        first, second = moments(rot_own, mq[j], vq[j])
        fq[j] = first
        sq[j] = second


def update_bias_kernel(sc, q0, q1, q2, q3, pb, mb, vb, gbias, sbias, nbias, full):
    half, k = pl.program_id(0), pl.program_id(1)

    @pl.when((half == 0) & (k == 0))
    def _():
        assemble(sc, (q0, q1, q2, q3), full)

    for i in range(DTILES):
        size = min(LANES, BPOS - i * LANES)
        at = (0, slice(None), slice(i * LANES, i * LANES + size))
        r = 3 * QROWS + (k * DTILES + i) * TYPES
        g = full[half, pl.ds(pl.multiple_of(r, TYPES), TYPES), 0:size].astype(f32)
        first, second = moments(g, mb[at], vb[at])
        gbias[at] = g
        sbias[at] = second
        w = pb[at]
        nbias[at] = w - table_rate * (step_of(first, second) + decay_rate * w)


def update_bias(sc, quarters, pb, mb, vb):
    block = pl.BlockSpec((1, TYPES, BPOS), lambda half, k: (half * HALF_HEADS + k, 0, 0))
    whole = pl.BlockSpec((TAIL // 2, LANES), lambda half, k: (0, 0))
    return pl.pallas_call(
        update_bias_kernel,
        out_shape=[jax.ShapeDtypeStruct(pb.shape, f32)] * 3,
        grid=(2, HALF_HEADS),
        in_specs=[SM] + [whole] * 4 + [block] * 3,
        out_specs=[block] * 3,
        scratch_shapes=[pltpu.VMEM((2, TAIL, LANES), bf16)],
        compiler_params=pltpu.CompilerParams(vmem_limit_bytes=60 * 2**20),
        cost_estimate=pl.CostEstimate(flops=0, bytes_accessed=0, transcendentals=0),
        name="update_bias",
    )(sc, *quarters, pb, mb, vb)


def body(
    tokens_in, target, loss_weight, shift_offsets, window_type, bias_index, owners, norm_params,
    w_qkv, w_proj, w_up, w_down, pos_bias, basis_qkv, basis_proj, basis_up, basis_down,
    m_qkv, v_qkv, m_proj, v_proj, m_up, v_up, m_down, v_down, m_bias, v_bias, m_norm, v_norm,
):
    rows = tokens_in.shape[0]
    n_win = lax.axis_size("win")
    block_cols = D // n_win
    me, tp = lax.axis_index("win"), lax.axis_index("tp")
    xb = (me >> 1) & 1
    sc = jnp.stack([me & 1, tp, xb]).astype(jnp.int32)
    total_rows = rows * n_win * lax.axis_size("tp")
    lw = loss_weight.reshape(rows, 1)
    wq = jnp.transpose(w_qkv, (1, 2, 0))
    pb = jnp.transpose(pos_bias, (2, 0, 1))
    mq, vq = jnp.transpose(m_qkv, (1, 0, 2)), jnp.transpose(v_qkv, (1, 0, 2))
    mp, vp, md, vd = m_proj.T, v_proj.T, m_down.T, v_down.T
    n_t = WTOK // ABLK
    idx = jnp.concatenate(
        [bias_index[:, :LANES].reshape(n_t, -1), bias_index[:, LANES:].reshape(n_t, -1)], axis=1
    )

    pad = -(-(block_cols + 3) // 16) * 16
    send_m, send_v = call(moments_kernel, [((pad, MCOLS), bf16)] * 2, [VM] * 9, name="moments")(
        lw, mq, mp, m_up, md, vq, vp, v_up, vd
    )
    a0, a1, b0, b1, town, tpar = call(
        pack_kernel,
        [((QROWS, D), bf16)] * 2
        + [((BROWS, D), bf16)] * 2
        + [((2 * TROWS, LOW), bf16)] * 2,
        [SM, SM] + [VM] * 5,
        [pltpu.VMEM((TROWS, LOW), f32)],
        name="pack",
    )(after(sc, send_m), window_type, wq, w_proj, w_up, w_down, pb)
    order = Order((a0,))
    all_m = lax.all_gather(send_m, "win", axis=0)
    all_v = lax.all_gather(send_v, "win", axis=0)
    pa0 = swap_tp(a0)
    ptab = swap_tp(tpar)

    attn_outs = [((rows, 2 * HROWS), bf16), ((3, rows, 2 * HROWS), bf16)]
    probs_out = [(PAIRS, f32)]
    tables = [pltpu.VMEM((TCOLS, WTOK, WTOK), f32)]
    mo, qkv_o, hid, probs_o = call(
        functools.partial(attend_kernel, True),
        attn_outs + [((rows, D), bf16)] + probs_out,
        [SM, SM] + [VM] * 6,
        tables,
        grid=(OWN_WIN,),
        out_specs=[VM] * 3 + [BY_WINDOW],
        name="attend_own",
    )(order(sc), shift_offsets.T, tokens_in, norm_params, a0, a1, town, idx)
    order.done(mo)

    pa0 = order(pa0)
    ptab = order(ptab)
    order.done(pa0, ptab)
    pa1 = permute_win(pa0, 1)
    pb0 = swap_tp(order(b0))
    mpar, qkv_p, probs_p = call(
        functools.partial(attend_kernel, False),
        attn_outs + probs_out,
        [SM, SM] + [VM] * 5,
        tables,
        grid=(OWN_WIN,),
        out_specs=[VM] * 2 + [BY_WINDOW],
        name="attend_partner",
    )(order(sc), shift_offsets.T, hid, pa0, pa1, ptab, idx)
    order.done(mpar)

    pb0 = order(pb0)
    pb1 = permute_win(pb0, 1)
    mean_parts = order(all_m)[:, block_cols : block_cols + 3, 0:LANES]
    result, s0, s1, dmid, dmo, dmp, small_two = call(
        mlp_kernel,
        [
            ((rows, D), bf16),
            ((2, BROWS, D), f32),
            ((2, BROWS, D), bf16),
            ((rows, D), f32),
            ((rows, 2 * HROWS), bf16),
            ((rows, 2 * HROWS), bf16),
            ((8, D), f32),
        ],
        [VM] * 12,
        [pltpu.VMEM((rows, 4 * HID), bf16), pltpu.VMEM((rows, 4 * HID), f32)],
        name="feed_forward",
    )(
        tokens_in, target, lw, mean_parts, swap_tp(mean_parts), norm_params,
        order(mo), mpar, b0, b1, pb0, pb1,
    )
    order.done(dmp)

    r1 = permute_win(s1, 1)
    par_sum = (s0[1] + r1[1].astype(f32)).astype(bf16)
    own_sum = s0[0] + r1[0].astype(f32)
    ry = swap_tp(par_sum)
    order.done(par_sum)

    ds_shape = (TCOLS, WTOK, WTOK)
    dx_scratch = pltpu.VMEM((rows, 3 * LOW), bf16)
    acc_scratch = pltpu.VMEM((TROWS, LOW), f32)
    gpar, gbp, dhid_p = call(
        back_partner_kernel,
        [((2, QROWS, D), bf16), ((TROWS, LOW), bf16), ((rows, D), f32)],
        [VM, VM, BY_WINDOW] + [VM] * 4,
        [pltpu.VMEM(ds_shape, f32), dx_scratch, acc_scratch],
        grid=(OWN_WIN,),
        name="back_partner",
    )(order(dmp), qkv_p, probs_p, pa0, pa1, hid, idx)
    got_b = swap_tp(gbp)
    got_a = swap_tp(gpar)
    order.done(gbp)

    main = own_sum + order(ry).astype(f32)
    send = cut_half(main, 1 - xb).astype(bf16)
    main = cut_half(main, xb)
    rx = permute_win(send, 2)
    order.done(send)

    go0, go1, dhid_o, ds_own = call(
        back_own_kernel,
        [((QROWS, D), f32)] * 2 + [((rows, D), f32), (PAIRS, f32)],
        [VM, VM, BY_WINDOW] + [VM] * 3,
        [dx_scratch],
        grid=(OWN_WIN,),
        out_specs=[VM] * 3 + [BY_WINDOW],
        name="back_own",
    )(order(dmo), qkv_o, probs_o, a0, a1, hid)
    order.done(go0)

    got_b = order(got_b)
    order.done(got_b)
    far = far_masks()
    main = (main + order(rx).astype(f32)).astype(bf16)
    rz = permute_win(main, far[0])
    order.done(main)

    grad_tokens, small_one = call(
        first_norm_kernel, [((rows, D), f32), ((8, D), f32)], [VM] * 5, name="first_norm"
    )(order(dhid_o), dhid_p, tokens_in, norm_params, dmid)
    small = jnp.concatenate([small_one[0:2], small_two[0:3], small_two[3:6]], axis=0)
    order.done(small)
    rs = swap_tp(small)

    cols = (owners[:, None] * block_cols + jnp.arange(block_cols)[None, :]).reshape(D, 1)
    own_cols = owners[me] * block_cols + jnp.arange(block_cols)[:, None]
    hi, lo, ohi, olo = call(
        order_kernel,
        [((4, D, D), bf16)] * 2 + [((4, block_cols, D), bf16)] * 2,
        [VM] * 6,
        name="order",
    )(order(cols), own_cols, basis_qkv, basis_proj, basis_up, basis_down)
    order.done(hi)
    small = small + order(rs)
    rs = permute_win(small, 1)
    order.done(small)

    for m, after_m in zip(far[:-1], far[1:]):
        main = (main.astype(f32) + order(rz).astype(f32)).astype(bf16)
        rz = permute_win(main, after_m)
        order.done(main)

    keep, send = call(
        back_bias_kernel,
        [((TAIL, LANES), f32)] * 2,
        [SM, SM] + [VM] * 6,
        [acc_scratch],
        name="back_bias",
    )(order(sc), window_type, ds_own.reshape(ds_shape), idx, go0, go1, got_a, got_b)
    order.done(send)

    main = (main.astype(f32) + order(rz).astype(f32)).astype(bf16)
    order.done(main)
    main_other = permute_win(main, 2)
    rt = permute_win(order(send), 1)
    small = small + order(rs)
    rs = permute_win(small, 2)
    order.done(small)

    tail = keep + order(rt)
    send = cut_half(tail, 1 - xb).astype(bf16)
    tail = cut_half(tail, xb)
    rt = permute_win(send, 2)
    order.done(send)

    small = small + order(rs)
    rs = permute_win(small, far[0])
    order.done(small)

    tail = (tail + order(rt).astype(f32)).astype(bf16)
    rt = permute_win(tail, far[0])
    order.done(tail)
    main_other = order(main_other)
    main = (main, main_other, permute_win(main, 1), permute_win(main_other, 1))
    for m in far[1:]:
        small = small + order(rs)
        rs = permute_win(small, m)
        order.done(small)
    for m in far[1:]:
        tail = (tail.astype(f32) + order(rt).astype(f32)).astype(bf16)
        rt = permute_win(tail, m)
        order.done(tail)

    def like(*arrays):
        return [(a.shape, f32) for a in arrays]

    (
        grad_proj, grad_up, grad_down, first_proj, second_proj, new_proj, copy_proj,
        first_up, second_up, new_up, copy_up, first_down, second_down, new_down, copy_down,
    ) = call(
        update_main_kernel,
        like(w_proj, w_up, w_down, mp, mp, w_proj) + [(w_proj.shape, bf16)]
        + like(m_up, m_up, w_up) + [(w_up.shape, bf16)]
        + like(md, md, w_down) + [(w_down.shape, bf16)],
        [SM] + [VM] * 19,
        [pltpu.VMEM((2, BROWS, D), bf16)],
        name="update_main",
    )(order(sc), *main, all_m, all_v, hi, lo, ohi, olo, w_proj, w_up, w_down, mp, vp, m_up, v_up, md, vd)

    order.done(grad_proj)
    tail = (tail.astype(f32) + order(rt).astype(f32)).astype(bf16)
    order.done(tail)
    tail_other = permute_win(tail, 2)
    small = small + order(rs)
    grad_norm = small[0:4]
    loss = jnp.sum(small[4]) * 0.5 / (total_rows * D)
    first_norm, second_norm = moments(grad_norm, m_norm, v_norm)
    new_norm = norm_params - table_rate * (step_of(first_norm, second_norm) + decay_rate * norm_params)
    order.done(new_norm, loss)
    tail_other = order(tail_other)
    tail = (tail, tail_other, permute_win(tail, 1), permute_win(tail_other, 1))
    grad_qkv, first_qkv, second_qkv, new_qkv, copy_qkv = call(
        update_qkv_kernel,
        like(wq, mq, mq, wq) + [(wq.shape, bf16)],
        [SM]
        + [VM] * 4
        + [pl.BlockSpec((n_win, pad, MBLK), lambda i: (0, 0, 0))] * 2
        + [pl.BlockSpec((1, D, D), lambda i: (0, 0, 0))] * 2
        + [pl.BlockSpec((1, block_cols, D), lambda i: (0, 0, 0))] * 2
        + [VM] * 3,
        [pltpu.VMEM((2, TAIL, LANES), bf16)],
        grid=(1,),
        name="update_qkv",
    )(order(sc), *tail, all_m, all_v, hi, lo, ohi, olo, wq, mq, vq)
    grad_bias, second_bias, new_bias = update_bias(
        sc, tail, pb, jnp.transpose(m_bias, (2, 0, 1)), jnp.transpose(v_bias, (2, 0, 1))
    )

    def wide(v):
        return jnp.transpose(v, (2, 0, 1))

    def heads_last(v):
        return jnp.transpose(v, (1, 2, 0))

    def rows_first(v):
        return jnp.transpose(v, (1, 0, 2))

    return (
        result,
        grad_tokens,
        loss,
        grad_norm,
        wide(grad_qkv),
        grad_proj,
        grad_up,
        grad_down,
        heads_last(grad_bias),
        rows_first(first_qkv),
        rows_first(second_qkv),
        wide(new_qkv),
        wide(copy_qkv),
        first_proj.T,
        second_proj.T,
        new_proj,
        copy_proj,
        first_up,
        second_up,
        new_up,
        copy_up,
        first_down.T,
        second_down.T,
        new_down,
        copy_down,
        heads_last(second_bias),
        heads_last(new_bias),
        second_norm,
        new_norm,
    )


def solution(mesh):
    return jax.shard_map(
        body,
        mesh=mesh,
        in_specs=(
            P(("win", "tp"), None),
            P(("win", "tp"), None),
            P(("win", "tp")),
            P("win", None),
            P("win"),
            P(),
            P(),
            P(),
            P(None, None, "tp"),
            P("tp", None),
            P(None, "tp"),
            P("tp", None),
            P(None, None, "tp"),
            P(),
            P(),
            P(),
            P(),
            P("win", None, "tp"),
            P("win", None, "tp"),
            P("tp", "win"),
            P("tp", "win"),
            P("win", "tp"),
            P("win", "tp"),
            P("tp", "win"),
            P("tp", "win"),
            P(None, None, "tp"),
            P(None, None, "tp"),
            P(),
            P(),
        ),
        out_specs=(
            P(("win", "tp"), None),
            P(("win", "tp"), None),
            P(),
            P(),
            P(None, None, "tp"),
            P("tp", None),
            P(None, "tp"),
            P("tp", None),
            P(None, None, "tp"),
            P("win", None, "tp"),
            P("win", None, "tp"),
            P(None, None, "tp"),
            P(None, None, "tp"),
            P("tp", "win"),
            P("tp", "win"),
            P("tp", None),
            P("tp", None),
            P("win", "tp"),
            P("win", "tp"),
            P(None, "tp"),
            P(None, "tp"),
            P("tp", "win"),
            P("tp", "win"),
            P("tp", None),
            P("tp", None),
            P(None, None, "tp"),
            P(None, None, "tp"),
            P(),
            P(),
        ),
        check_vma=False,
    )
```
